32 devices in a mesh: inst: 4 (over y, x), tp: 8 (over z, core).
Axes of the slice: x: 2, y: 2, z: 4, core: 2. Of those that a mesh axis runs over, the one named last changes fastest.
Arguments:
- tokens: bfloat16 [640, 8192], P('inst'), as said below
- doc_ids: int32 [4, 160], replicated, may hold values from 0 to 3, never falling along the last dimension, each value on 1 to 80 neighbouring positions
- query_one: bfloat16 [8192, 1024], P('inst', 'tp'), as said below
- keyval_one: bfloat16 [8192, 256], P('inst', 'tp'), as said below
- output_one: bfloat16 [1024, 8192], P('tp', 'inst'), may hold values from -0.1875 to 0.1875
- query_two: bfloat16 [8192, 1024], P('inst', 'tp'), as said below
- keyval_two: bfloat16 [8192, 256], P('inst', 'tp'), as said below
- output_two: bfloat16 [1024, 8192], P('tp', 'inst'), may hold values from -0.25 to 0.25
Outputs:
- blended: bfloat16 [640, 8192], P('inst', 'tp')
The draws below stay inside these ranges and needn't reach their ends.
Inputs may be any that keep to these rules, and one draw needn't show every extreme that they name: `doc_ids`: along each row the document numbers never fall; each document holds 1 to 80 positions. `query_one`: A projection scaled by the square root of its fan-in. `keyval_one`: A projection scaled by the square root of its fan-in. `query_two`: A projection scaled by the square root of its fan-in. `keyval_two`: A projection scaled by the square root of its fan-in. `tokens`: hidden rows of order one.
All inputs are finite; a program needn't handle non-finite values.
Results may differ from the reference program's by a relative error of at most 0.034.
Values may be sent and summed in bfloat16 or wider, within the bound.
No kernel may reach another device: no remote copies, remote signals or barrier semaphores. Data moves between devices by JAX's collectives and lax.ppermute only.
A program may use at most 64 MiB of HBM per device.

```python
import math
import jax
import jax.numpy as jnp
import numpy as np
from jax import lax

D = 8192
HD = 128
GROUP = 8
TOK_INST = 160
DOCS = 4
TOKENS = 640
HQ = 8
KVH = 1
MOST = 80
N_INST = 4
N_TP = 8


def query_law(key):
    noise = jax.random.normal(key, (D, HQ, HD), jnp.float32) * D ** (-0.5)
    mixed = noise
    return mixed.reshape(D, HQ * HD).astype(jnp.bfloat16)


def keyval_law(key):
    noise = jax.random.normal(key, (D, KVH, 2, HD), jnp.float32) * D ** (-0.5)
    key_part = noise[:, :, 0]
    both = jnp.stack([key_part, noise[:, :, 1]], axis=2)
    return both.reshape(D, KVH * 2 * HD).astype(jnp.bfloat16)


def draw_tokens(key, part):
    key = jax.random.fold_in(key, 3)
    first, second, third = jax.random.split(key, 3)
    row_scale = jnp.exp(jax.random.uniform(first, (TOKENS, 1), jnp.float32, -1.15, 1.15))
    col_scale = jnp.exp(jax.random.uniform(second, (1, D), jnp.float32, -1.15, 1.15))
    base = jax.random.normal(third, (TOKENS, D), jnp.float32)
    return (0.5 * base * row_scale * col_scale).astype(jnp.bfloat16)


def draw_query_one(key, part):
    key = jax.random.fold_in(key, 21)
    return query_law(key)


def draw_keyval_one(key, part):
    key = jax.random.fold_in(key, 22)
    return keyval_law(key)


def draw_query_two(key, part):
    key = jax.random.fold_in(key, 23)
    return query_law(key)


def draw_keyval_two(key, part):
    key = jax.random.fold_in(key, 24)
    return keyval_law(key)


def raised(entries, key, source, target, shards_of, factor):
    owner, partner = [(jnp.arange(entries.shape[dim]) // (entries.shape[dim] // shards_of)).reshape([-1 if axis == dim else 1 for axis in range(entries.ndim)]) for dim in (source, target)]
    chosen = jax.random.permutation(key, shards_of)[partner]
    strong = (owner == chosen) | (owner == (partner + shards_of // 2) % shards_of)
    return jnp.where(strong, factor * entries, entries)


def shard_levels(stream_key, extent, cuts, least, largest):
    loudness = 1.0
    for dim, shards_of in cuts:
        draws = jax.random.uniform(jax.random.fold_in(jax.random.fold_in(stream_key, 6), dim), (shards_of,), jnp.float32, least / len(cuts), largest / len(cuts))
        loudness = loudness * jnp.repeat(jnp.exp(draws), extent[dim] // shards_of).reshape((-1,) + (1,) * (len(extent) - 1 - dim))
    return loudness


def split_up(amount, total, bound, slope):
    weights = [(1 << 20) // math.isqrt(standing ** slope) + 1 for standing in range(2, amount + 1)]
    surplus, counts = total - bound - (amount - 1), [1] * (amount - 1)
    while surplus > 0:
        movable = [i for i in range(amount - 1) if counts[i] < bound]
        whole, budget = sum([weights[i] for i in movable]), surplus
        for i in movable:
            more = min(bound - counts[i], max(1, budget * weights[i] // whole), surplus)
            counts[i] = counts[i] + more
            surplus = surplus - more
    return np.array([bound] + counts)


def ragged(own_key, amount, total, reach, skew):
    if amount == 2:
        one = jax.random.randint(own_key, (), max(1, total - reach), min(reach, total - 1) + 1)
        return jnp.stack([one, total - one])
    lengths = jnp.asarray(split_up(amount, total, reach, skew), jnp.int32)
    couples = (amount - 1) // 2
    donor, sink = lengths[1:1 + 2 * couples:2], lengths[2:2 + 2 * couples:2]
    room = jnp.minimum(donor - 1, reach - sink)
    moved = jax.random.randint(jax.random.fold_in(own_key, 1), (couples,), 0, 1 << 20) % (room + 1)
    lengths = lengths.at[1:1 + 2 * couples:2].set(donor - moved).at[2:2 + 2 * couples:2].set(sink + moved)
    return lengths[jax.random.permutation(jax.random.fold_in(own_key, 2), amount)]


def normal_values(key, dims, width, reach, cuts=(), kind=jnp.bfloat16):
    level = shard_levels(key, dims, cuts, -0.22, 0.18) if cuts else 1.0
    values = jax.random.normal(key, dims, jnp.float32) * width * level
    return jnp.minimum(jnp.maximum(values, -reach), reach).astype(kind)


def heavy_noise(own_key, extent, spread, limit, pieces, heavy, kind=jnp.bfloat16):
    values = spread * jax.random.normal(own_key, extent, jnp.float32)
    if pieces:
        values = values * shard_levels(own_key, extent, pieces, -0.22, 0.18)
    return jnp.clip(raised(values, jax.random.fold_in(own_key, 3), *heavy), -limit, limit).astype(kind)


def setup_inputs(seed: int = 0) -> dict:
    keys = jax.random.split(jax.random.key(seed), 9)
    return {
        "tokens": draw_tokens(jax.random.fold_in(keys[8], 71), 0),
        "doc_ids": jax.vmap(lambda own: jnp.searchsorted(jnp.cumsum(ragged(own, DOCS, TOK_INST, MOST, 2)), jnp.arange(TOK_INST), side="right"))(jax.random.split(keys[1], N_INST)).reshape((N_INST, TOK_INST)).astype(jnp.int32),
        "query_one": draw_query_one(jax.random.fold_in(keys[8], 71), 0),
        "keyval_one": draw_keyval_one(jax.random.fold_in(keys[8], 71), 0),
        "output_one": normal_values(keys[4], (HQ * HD, D), (HQ * HD) ** -0.5, 0.1875, ((0, 8), (1, 4))),
        "query_two": draw_query_two(jax.random.fold_in(keys[8], 71), 0),
        "keyval_two": draw_keyval_two(jax.random.fold_in(keys[8], 71), 0),
        "output_two": heavy_noise(keys[7], (HQ * HD, D), (HQ * HD) ** -0.5, 0.25, ((0, 8), (1, 4)), (0, 1, 8, 2.0)),
    }


def normalize(hidden):
    floats = hidden.astype(jnp.float32)
    scale = lax.rsqrt(lax.optimization_barrier(jnp.mean(floats * floats, axis=1, keepdims=True)) + 1e-06)
    return (floats * scale).astype(jnp.bfloat16)

def attend(hidden, docs, query_weight, keyval_weight, output_weight):
    normed = normalize(hidden)
    queries = (jnp.dot(normed, query_weight, preferred_element_type=jnp.float32) * HD ** (-0.5)).astype(jnp.bfloat16)
    keyvals = jnp.dot(normed, keyval_weight, preferred_element_type=jnp.float32).astype(jnp.bfloat16)
    query_rows = queries.reshape(N_INST, TOK_INST, HQ, HD).astype(jnp.float32)
    split_kv = keyvals.reshape(N_INST, TOK_INST, KVH, 2, HD).astype(jnp.float32)
    key_rows = jnp.repeat(split_kv[:, :, :, 0], GROUP, axis=2)
    value_rows = jnp.repeat(split_kv[:, :, :, 1], GROUP, axis=2)
    scores = jnp.einsum('ntha,nsha->nhts', query_rows, key_rows, precision=lax.Precision.HIGHEST)
    position = jnp.arange(TOK_INST)
    allowed = (docs[:, :, None] == docs[:, None, :]) & (position[None, None, :] <= position[None, :, None])
    scores = jnp.where(allowed[:, None], scores, -1e+30)
    row_top = lax.optimization_barrier(jnp.max(scores, axis=3, keepdims=True))
    weights = jnp.exp(scores - row_top)
    probabilities = (weights / lax.optimization_barrier(jnp.sum(weights, axis=3, keepdims=True))).astype(jnp.bfloat16)
    context = jnp.einsum('nhts,nsha->ntha', probabilities.astype(jnp.float32), value_rows, precision=lax.Precision.HIGHEST)
    context = context.astype(jnp.bfloat16).reshape(TOKENS, HQ * HD)
    per_rank = HQ * HD // N_TP
    context_groups = context.reshape(TOKENS, N_TP, per_rank).transpose(1, 0, 2)
    output_groups = output_weight.reshape(N_TP, per_rank, D)

    def add_group(total, pair):
        term = jnp.dot(pair[0], pair[1], preferred_element_type=jnp.float32)
        rounded = lax.optimization_barrier(term.astype(jnp.bfloat16))
        return (total + rounded.astype(jnp.float32), None)
    total, unused = lax.scan(add_group, jnp.zeros((TOKENS, D), jnp.float32), (context_groups, output_groups))
    return total

def reference(tokens, doc_ids, query_one, keyval_one, output_one, query_two, keyval_two, output_two):
    attended_one = attend(tokens, doc_ids, query_one, keyval_one, output_one)
    middle = (tokens.astype(jnp.float32) + attended_one).astype(jnp.bfloat16)
    arrived = jnp.roll(middle, TOK_INST, axis=0)
    arrived_docs = jnp.roll(doc_ids, 1, axis=0)
    attended_two = attend(arrived, arrived_docs, query_two, keyval_two, output_two)
    return (arrived.astype(jnp.float32) + attended_two).astype(jnp.bfloat16)
```

```python
import functools
import math

import jax
import jax.numpy as jnp
from jax import lax
from jax.experimental import pallas as pl
from jax.experimental.pallas import tpu as pltpu
from jax.sharding import PartitionSpec as P

GROUP = 8
EPS = 1e-6
LANES = 128
VMEM = pl.BlockSpec(memory_space=pltpu.VMEM)
HBM = pl.BlockSpec(memory_space=pltpu.MemorySpace.HBM)
LAST = pl.BlockSpec(memory_space=pltpu.VMEM)


def contract(left, right, dims):
    return lax.dot_general(left, right, ((dims[:1], dims[1:]), ((), ())), preferred_element_type=jnp.float32)


def after(value, *others):
    return lax.optimization_barrier((value, others))[0]


def exchange(block, axis, groups=None):
    return lax.all_to_all(block, axis, 0, 0, axis_index_groups=groups)


def other_core(block):
    count = lax.axis_size("tp")
    return lax.ppermute(block, "tp", [(s, s ^ 1) for s in range(count)])


def own_core():
    return lax.rem(lax.axis_index("tp"), 2)


def transposed(block, rows):
    row = lax.broadcasted_iota(jnp.int32, (rows, block.shape[1]), 0)
    column = lax.broadcasted_iota(jnp.int32, (rows, block.shape[1]), 1)
    pick = (row == column).astype(jnp.bfloat16)
    return contract(pick, block, (1, 1)).astype(jnp.bfloat16)


def call(kernel, name, outs, ins, args, scratch=(), places=None):
    places = places or [VMEM] * len(outs)
    held = [value for value, spec in zip([*args, *outs], [*ins, *places]) if spec is VMEM]
    total = sum(math.prod(value.shape) * value.dtype.itemsize for value in held)
    work = sum(math.prod(ref.shape) * ref.dtype.itemsize for ref in scratch if hasattr(ref.dtype, "itemsize"))
    resident = total <= 16 * 2**20
    if resident:
        spaces = [spec.memory_space for spec in ins]
        args = [pltpu.with_memory_space_constraint(value, space) for value, space in zip(args, spaces)]
        outs = [out if spec is LAST else spec.memory_space(out.shape, out.dtype) for out, spec in zip(outs, places)]
        limit = work + 12 * 2**20
    else:
        limit = 56 * 2**20
    return pl.pallas_call(
        kernel,
        out_shape=outs,
        in_specs=ins,
        out_specs=[VMEM if spec is LAST else spec for spec in places],
        scratch_shapes=list(scratch),
        compiler_params=pltpu.CompilerParams(vmem_limit_bytes=limit),
        name=name,
    )(*args)


def bfloat(*shape):
    return jax.ShapeDtypeStruct(shape, jnp.bfloat16)


def shifted(block, axis, distance):
    count = lax.axis_size(axis)
    return lax.ppermute(block, axis, [(s, (s + distance) % count) for s in range(count)])


def core_groups():
    ranks = lax.axis_size("tp")
    return [list(range(core, ranks, 2)) for core in range(2)]


def cut_kernel(tokens, shard, output, keyval, sent, bound, held, sems):
    count, both, width = sent.shape
    head = output.shape[0]
    sub = shard.shape[0] // count
    half = both - sub
    start = pl.multiple_of(own_core() * half, half)
    copies = [
        pltpu.make_async_copy(output, held.at[pl.ds(0, head), :], sems.at[2, 0]),
        pltpu.make_async_copy(keyval, held.at[pl.ds(head, keyval.shape[0]), :], sems.at[2, 1]),
    ]
    for q in range(count):
        source = tokens.at[pl.ds(start, half), pl.ds(q * width, width)]
        copies.append(pltpu.make_async_copy(source, sent.at[q, pl.ds(0, half)], sems.at[0, q]))
        source = shard.at[pl.ds(q * sub, sub), :]
        copies.append(pltpu.make_async_copy(source, sent.at[q, pl.ds(half, sub)], sems.at[1, q]))
    for copy in copies:
        copy.start()
    for copy in copies[:2]:
        copy.wait()
    save = pltpu.make_async_copy(held, bound, sems.at[2, 2])
    save.start()
    for copy in copies[2:]:
        copy.wait()
    save.wait()


def cut(tokens, shard, output, keyval, count):
    rows, depth = tokens.shape
    together = (output.shape[0] + keyval.shape[0], output.shape[1])
    outs = [bfloat(count, rows // 2 + shard.shape[0] // count, depth // count), bfloat(*together)]
    scratch = [pltpu.VMEM(together, jnp.bfloat16), pltpu.SemaphoreType.DMA((3, max(3, count)))]
    return call(cut_kernel, "cut", outs, [HBM] * 4, [tokens, shard, output, keyval], scratch, [VMEM, HBM])


def norm_kernel(tokens, scale, whole, sems):
    pieces = sems.shape[0]
    step = tokens.shape[1] // pieces
    copies = []
    for p in range(pieces):
        columns = pl.ds(p * step, step)
        copies.append(pltpu.make_async_copy(tokens.at[:, columns], whole.at[:, columns], sems.at[p]))
    for copy in copies:
        copy.start()
    total = jnp.zeros((tokens.shape[0], LANES), jnp.float32)
    for p, copy in enumerate(copies):
        copy.wait()
        for low in range(p * step, (p + 1) * step, LANES):
            floats = whole[:, low : low + LANES].astype(jnp.float32)
            total = total + floats * floats
    squares = jnp.sum(total, axis=1, keepdims=True)
    scale[...] = lax.rsqrt(squares / tokens.shape[1] + EPS)


def norms(tokens):
    outs = [jax.ShapeDtypeStruct((tokens.shape[0], 1), jnp.float32)]
    scratch = [pltpu.VMEM(tokens.shape, jnp.bfloat16), pltpu.SemaphoreType.DMA((4,))]
    return call(norm_kernel, "norms", outs, [HBM], [tokens], scratch)[0]


def part_kernel(got, mine):
    for q in range(mine.shape[0]):
        mine[q] = got[q, : mine.shape[1], :]


def part(got, half):
    return call(part_kernel, "part", [bfloat(got.shape[0], half, got.shape[2])], [VMEM], [got])[0]


def aim_kernel(got, heads, *pieces):
    planes = len(pieces)
    for e, piece in enumerate(pieces):
        half = got.shape[1] - piece.shape[0]
        piece[...] = got[lax.rem(lax.axis_index("tp") // 2 + e, planes), half:, :]


def aim(got, half, heads):
    planes = heads.shape[0]
    outs = [bfloat(got.shape[1] - half, got.shape[2])] * planes
    return call(aim_kernel, "aim", outs, [VMEM, VMEM], [got, heads])


def keep_kernel(source, output, *refs):
    pieces, (kept, rows) = refs[:-2], refs[-2:]
    kept[...] = source[...]
    for e, piece in enumerate(pieces):
        rows[e] = piece[...]


def keep(block, output, pieces):
    outs = [bfloat(*block.shape), bfloat(len(pieces), *pieces[0].shape)]
    ins = [VMEM, HBM] + [VMEM] * len(pieces)
    return call(keep_kernel, "keep", outs, ins, [block, output, *pieces], places=[VMEM, LAST])


def fill_tall(keyval, tall):
    piece = keyval.shape[0]
    tall[:piece, :] = keyval[...]
    tall[piece:, :] = jnp.zeros((LANES - piece, tall.shape[1]), tall.dtype)


def project_kernel(mine, other, query, keyval, saved, sums, held, tall, sem):
    count, half, _ = mine.shape
    core = own_core()
    for q in range(count):
        for source, place in ((mine, core), (other, 1 - core)):
            held[pl.ds(pl.multiple_of((2 * q + place) * half, half), half), :] = source[q]
    save = pltpu.make_async_copy(held, saved, sem)
    save.start()
    fill_tall(keyval, tall)
    hidden = held[...]
    head = query.shape[1]
    queries = jnp.dot(hidden, query[...], preferred_element_type=jnp.float32).astype(jnp.bfloat16)
    products = contract(hidden, tall[...], (1, 1)).astype(jnp.bfloat16)
    for q in range(count):
        sums[q, :, :head] = queries[2 * q * half : 2 * (q + 1) * half]
        sums[q, :, head:] = products[2 * q * half : 2 * (q + 1) * half]
    save.wait()


def project(mine, other, query, keyval):
    count, half, width = mine.shape
    rows = 2 * half
    outs = [bfloat(count * rows, width), bfloat(count, rows, query.shape[1] + LANES)]
    scratch = [
        pltpu.VMEM((count * rows, width), jnp.bfloat16),
        pltpu.VMEM((LANES, width), jnp.bfloat16),
        pltpu.SemaphoreType.DMA(()),
    ]
    args = [mine, other, query, keyval]
    return call(project_kernel, "project", outs, [VMEM] * 4, args, scratch, [HBM, VMEM])


def summed(parts):
    total = parts[0].astype(jnp.float32)
    for part in parts[1:]:
        total = total + part.astype(jnp.float32)
    return total


def finish_kernel(parts, scale, queries, keyvals_t):
    head = queries.shape[1]
    total = summed([parts[q] for q in range(parts.shape[0])]) * scale[...]
    queries[...] = (total[:, :head] * head ** (-0.5)).astype(jnp.bfloat16)
    piece = transposed(total[:, head:].astype(jnp.bfloat16), keyvals_t.shape[1])
    for g in range(keyvals_t.shape[0]):
        keyvals_t[g] = piece


def finish(parts, scale, head, piece):
    rows = parts.shape[1]
    outs = [bfloat(rows, head), bfloat(GROUP, piece, rows)]
    return call(finish_kernel, "finish", outs, [VMEM] * 2, [parts, scale])


def attention(queries, keys_t, values_t, dims, doc_ids, back):
    rows = queries.shape[0]
    at = lax.broadcasted_iota(jnp.int32, (rows, rows), 0)
    key_at = lax.broadcasted_iota(jnp.int32, (rows, rows), 1)
    count = doc_ids.shape[0]
    own = lax.rem(lax.axis_index("inst") - back + count, count)
    docs_row = jnp.broadcast_to(doc_ids[pl.ds(own, 1), :].astype(jnp.float32), (rows, rows))
    docs_column = jnp.sum(jnp.where(at == key_at, docs_row, 0.0), axis=1, keepdims=True)
    allowed = (docs_column == docs_row) & (key_at <= at)
    scores = contract(queries, keys_t, (1, dims[0]))
    scores = jnp.where(allowed, scores, -1e30)
    weights = jnp.exp(scores - jnp.max(scores, axis=1, keepdims=True))
    probabilities = weights / jnp.sum(weights, axis=1, keepdims=True)
    return contract(probabilities.astype(jnp.bfloat16), values_t, (1, dims[1])).astype(jnp.bfloat16)


def first_kernel(queries, doc_ids, pieces, context):
    span = pieces.shape[0] // 2
    keys_t = jnp.concatenate([pieces[g] for g in range(span)], 0)
    values_t = jnp.concatenate([pieces[g] for g in range(span, 2 * span)], 0)
    result = attention(queries[...], keys_t, values_t, (0, 1), doc_ids, 0)
    for z in range(context.shape[0]):
        context[z] = result


def first_attend(queries, doc_ids, pieces):
    outs = [bfloat(lax.axis_size("tp") // 2, *queries.shape)]
    return call(first_kernel, "attend", outs, [VMEM] * 3, [queries, doc_ids, pieces])[0]


def second_kernel(depth, head, rows, parts, doc_ids, sent):
    wide = 3 * head
    total = summed([parts[q, :rows, :wide] for q in range(parts.shape[0])])
    high = summed([parts[q, rows : rows + 16, :] for q in range(parts.shape[0])])
    across = jnp.broadcast_to(high[0:1] + high[1:2], (rows, parts.shape[2]))
    at = lax.broadcasted_iota(jnp.int32, across.shape, 0)
    lane = lax.broadcasted_iota(jnp.int32, across.shape, 1)
    squares = jnp.sum(jnp.where(at == lane, across, 0.0), axis=1, keepdims=True)
    total = total * lax.rsqrt(squares / depth + EPS)
    queries = (total[:, :head] * head ** (-0.5)).astype(jnp.bfloat16)
    keys = total[:, head : 2 * head].astype(jnp.bfloat16)
    values = total[:, 2 * head :].astype(jnp.bfloat16)
    result = attention(queries, keys, values, (1, 0), doc_ids, 1)
    for z in range(sent.shape[0]):
        sent[z, :, :head] = result
        sent[z, :, head:] = parts[z, :rows, wide:]


def second_attend(parts, doc_ids, depth, head):
    rows = doc_ids.shape[1]
    outs = [bfloat(parts.shape[0], rows, parts.shape[2] - 2 * head)]
    kernel = functools.partial(second_kernel, depth, head, rows)
    return call(kernel, "attend", outs, [VMEM] * 2, [parts, doc_ids])[0]


def spread_kernel(heads, sent):
    for q in range(sent.shape[0]):
        sent[q] = heads[...]


def spread(heads):
    outs = [bfloat(lax.axis_size("inst"), *heads.shape)]
    return call(spread_kernel, "spread", outs, [VMEM], [heads])[0]


def spans(count):
    return [range(low, min(low + 4, count)) for low in range(0, count, 4)]


def place_contexts(mine, other, left, span):
    _, pairs, rows, head = mine.shape
    core = own_core()
    for source, parity in ((mine, core), (other, 1 - core)):
        for e in range(pairs):
            columns = pl.ds(pl.multiple_of((2 * e + parity) * head, head), head)
            for at, q in enumerate(span):
                left[at * rows : (at + 1) * rows, columns] = source[q, e]


def advance_kernel(step, before, mine, other, output, query, sums, left, held, tall, hidden, blended, sems):
    count, pairs, rows, head = mine.shape
    width = before.shape[1]
    ranks = 2 * pairs
    first = lax.axis_index("tp") // GROUP * GROUP
    copies = []
    for at in range(width // step):
        columns = pl.ds(at * step, step)
        pairs_of = [
            (output.at[:, pl.ds(0, head), columns], held.at[:, :, columns]),
            (before.at[:, columns], hidden.at[:, columns]),
            (output.at[pl.ds(first, GROUP), pl.ds(head, tall.shape[1]), columns], tall.at[:, :, columns]),
        ]
        copies.append([pltpu.make_async_copy(*pair, sems.at[c, at]) for c, pair in enumerate(pairs_of)])
    for chunk in copies:
        for copy in chunk:
            copy.start()
    for span in spans(count):
        place_contexts(mine, other, left, span)
        low, high = span[0] * rows, (span[-1] + 1) * rows
        queries, keyvals, squares = 0.0, 0.0, 0.0
        for at, chunk in enumerate(copies):
            if span[0] == 0:
                for copy in chunk:
                    copy.wait()
            columns = pl.ds(at * step, step)
            right = held[:, :, columns].reshape(ranks * head, step)
            attended = jnp.dot(left[: high - low, :], right, preferred_element_type=jnp.float32)
            after_one = (hidden[low:high, columns].astype(jnp.float32) + attended).astype(jnp.bfloat16)
            blended[low:high, columns] = after_one
            queries = queries + jnp.dot(after_one, query[columns, :], preferred_element_type=jnp.float32)
            right = tall[:, :, columns].reshape(GROUP * tall.shape[1], step)
            keyvals = keyvals + contract(after_one, right, (1, 1))
            floats = after_one.astype(jnp.float32)
            squares = squares + jnp.sum(floats * floats, axis=1, keepdims=True)
        queries, keyvals = queries.astype(jnp.bfloat16), keyvals.astype(jnp.bfloat16)
        for at, q in enumerate(span):
            slot = (q + 1) % count
            block = slice(at * rows, (at + 1) * rows)
            sums[slot, :rows, :head] = queries[block]
            sums[slot, :rows, head : 3 * head] = keyvals[block]
            lanes = sums.shape[2]
            row = lax.broadcasted_iota(jnp.int32, (rows, lanes), 0)
            lane = lax.broadcasted_iota(jnp.int32, (rows, lanes), 1)
            square = jnp.where(row == lane, squares[block], 0.0)
            square = jnp.sum(square, axis=0, keepdims=True)
            high_part = square.astype(jnp.bfloat16).astype(jnp.float32)
            row = lax.broadcasted_iota(jnp.int32, (16, lanes), 0)
            extra = jnp.where(row == 0, high_part, jnp.where(row == 1, square - high_part, 0.0))
            sums[slot, rows:, :] = extra.astype(jnp.bfloat16)
    wide = 3 * head
    slim = (sums.shape[2] - wide) // 2
    for r in range(ranks):

        @pl.when(lax.axis_index("tp") == r)
        def give():
            for b in range(2):
                low = b * (width // 2) + r * slim
                for q in range(count):
                    block = blended[q * rows : (q + 1) * rows, low : low + slim]
                    sums[(q + 1) % count, :rows, wide + b * slim : wide + (b + 1) * slim] = block


def advance(before, mine, other, output, query):
    count, pairs, rows, head = mine.shape
    total, width = before.shape
    step = min(512, width)
    ranks, both, _ = output.shape
    scratch = [
        pltpu.VMEM((min(4, count) * rows, ranks * head), jnp.bfloat16),
        pltpu.VMEM((ranks, head, width), jnp.bfloat16),
        pltpu.VMEM((GROUP, both - head, width), jnp.bfloat16),
        pltpu.VMEM((total, width), jnp.bfloat16),
        pltpu.VMEM((total, width), jnp.bfloat16),
        pltpu.SemaphoreType.DMA((3, width // step)),
    ]
    outs = [bfloat(count, rows + 16, 3 * head + width // ranks)]
    ins = [HBM] + [VMEM] * 2 + [HBM, VMEM]
    args = [before, mine, other, output, query]
    return call(functools.partial(advance_kernel, step), "advance", outs, ins, args, scratch)[0]


def blend_kernel(got, rows_by, kept, sent, held, sems):
    pairs, rows, _ = got.shape
    count, _, sub, _ = rows_by.shape
    head = count * sub
    plane = lax.axis_index("tp") // 2
    copies = []
    for i in range(count):
        for e in range(pairs):
            target = held.at[pl.ds(e * head + i * sub, sub), :]
            copies.append(pltpu.make_async_copy(rows_by.at[i, e], target, sems.at[i, e]))
    for copy in copies:
        copy.start()
    left = jnp.concatenate([got[lax.rem(plane - e + pairs, pairs), :, :head] for e in range(pairs)], 1)
    half = kept.shape[1]
    slim = half // (2 * pairs)
    for copy in copies:
        copy.wait()
    for core in range(2):

        @pl.when(own_core() == core)
        def give():
            for b in range(2):
                rest = []
                for a in range(pairs):
                    ours = got[a, :, head + b * slim : head + (b + 1) * slim]
                    rest += [ours, jnp.zeros_like(ours)] if core == 0 else [jnp.zeros_like(ours), ours]
                rest = jnp.concatenate(rest, 1).astype(jnp.float32)
                right = held[:, b * half : (b + 1) * half]
                total = jnp.dot(left, right, preferred_element_type=jnp.float32) + rest
                if b == core:
                    kept[...] = total
                else:
                    sent[...] = total.astype(jnp.bfloat16)


def blend(got, rows_by):
    pairs, rows, _ = got.shape
    count, _, sub, width = rows_by.shape
    scratch = [pltpu.VMEM((pairs * count * sub, width), jnp.bfloat16), pltpu.SemaphoreType.DMA((count, pairs))]
    outs = [jax.ShapeDtypeStruct((rows, width // 2), jnp.float32), bfloat(rows, width // 2)]
    return call(blend_kernel, "blend", outs, [VMEM, HBM], [got, rows_by], scratch)


def join_kernel(kept, arrived, blended):
    blended[...] = (kept[...] + arrived[...].astype(jnp.float32)).astype(jnp.bfloat16)


def join(kept, arrived):
    return call(join_kernel, "join", [bfloat(*kept.shape)], [VMEM] * 2, [kept, arrived], places=[LAST])[0]


def shards(tokens, doc_ids, query_one, keyval_one, output_one, query_two, keyval_two, output_two):
    count, ranks = lax.axis_size("inst"), lax.axis_size("tp")
    rows, depth = tokens.shape
    head, piece = query_one.shape[1], keyval_one.shape[1]
    groups = None
    if ranks > GROUP:
        groups = [list(range(low, low + GROUP)) for low in range(0, ranks, GROUP)]

    sent, bound = cut(tokens, output_two, output_one, keyval_two.T, count)
    output_all = lax.all_gather(bound, "tp", axis=0)
    got = exchange(sent, "inst")
    mine = part(got, rows // 2)
    held, sums = project(mine, other_core(mine), query_one, keyval_one.T)
    queries, keyvals_t = finish(exchange(sums, "inst"), norms(tokens), head, piece)
    context = first_attend(queries, doc_ids, exchange(keyvals_t, "tp", groups))
    heads = exchange(context, "tp", core_groups())
    pieces = aim(got, rows // 2, heads)
    pieces = [pieces[0]] + [shifted(pieces[e], "tp", 2 * e) for e in range(1, ranks // 2)]
    mine, rows_by = keep(exchange(spread(heads), "inst"), output_all, pieces)
    rows_by = lax.all_gather(rows_by, "inst", axis=0)
    sums = advance(held, mine, other_core(mine), output_all, query_two)

    sent = second_attend(exchange(sums, "inst"), doc_ids, depth, head)
    kept, sent = blend(exchange(sent, "tp", core_groups()), rows_by)
    return join(kept, other_core(sent))


def solution(mesh):
    placed = (
        P("inst", None),
        P(),
        P("inst", "tp"),
        P("inst", "tp"),
        P("tp", "inst"),
        P("inst", "tp"),
        P("inst", "tp"),
        P("tp", "inst"),
    )
    return jax.shard_map(
        shards, mesh=mesh, in_specs=placed, out_specs=P("inst", "tp"), check_vma=False
    )
```

```python
import functools
import math

import jax
import jax.numpy as jnp
from jax import lax
from jax.experimental import pallas as pl
from jax.experimental.pallas import tpu as pltpu
from jax.sharding import PartitionSpec as P

GROUP = 8
EPS = 1e-6
LANES = 128
VMEM = pl.BlockSpec(memory_space=pltpu.VMEM)
HBM = pl.BlockSpec(memory_space=pltpu.MemorySpace.HBM)
LAST = pl.BlockSpec(memory_space=pltpu.VMEM)


def contract(left, right, dims):
    return lax.dot_general(left, right, ((dims[:1], dims[1:]), ((), ())), preferred_element_type=jnp.float32)


def exchange(block, axis, groups=None):
    return lax.all_to_all(block, axis, 0, 0, axis_index_groups=groups)


def other_core(block):
    count = lax.axis_size("tp")
    return lax.ppermute(block, "tp", [(s, s ^ 1) for s in range(count)])


def own_core():
    return lax.rem(lax.axis_index("tp"), 2)


def transposed(block, rows):
    row = lax.broadcasted_iota(jnp.int32, (rows, block.shape[1]), 0)
    column = lax.broadcasted_iota(jnp.int32, (rows, block.shape[1]), 1)
    pick = (row == column).astype(jnp.bfloat16)
    return contract(pick, block, (1, 1)).astype(jnp.bfloat16)


def call(kernel, name, outs, ins, args, scratch=(), places=None):
    places = places or [VMEM] * len(outs)
    held = [value for value, spec in zip([*args, *outs], [*ins, *places]) if spec is VMEM]
    total = sum(math.prod(value.shape) * value.dtype.itemsize for value in held)
    work = sum(math.prod(ref.shape) * ref.dtype.itemsize for ref in scratch if hasattr(ref.dtype, "itemsize"))
    resident = total <= 16 * 2**20
    if resident:
        spaces = [spec.memory_space for spec in ins]
        args = [pltpu.with_memory_space_constraint(value, space) for value, space in zip(args, spaces)]
        outs = [out if spec is LAST else spec.memory_space(out.shape, out.dtype) for out, spec in zip(outs, places)]
        limit = work + 12 * 2**20
    else:
        limit = 56 * 2**20
    return pl.pallas_call(
        kernel,
        out_shape=outs,
        in_specs=ins,
        out_specs=[VMEM if spec is LAST else spec for spec in places],
        scratch_shapes=list(scratch),
        compiler_params=pltpu.CompilerParams(vmem_limit_bytes=limit),
        name=name,
    )(*args)


def bfloat(*shape):
    return jax.ShapeDtypeStruct(shape, jnp.bfloat16)


def shifted(block, axis, distance):
    count = lax.axis_size(axis)
    return lax.ppermute(block, axis, [(s, (s + distance) % count) for s in range(count)])


def core_groups():
    ranks = lax.axis_size("tp")
    return [list(range(core, ranks, 2)) for core in range(2)]


def cut_kernel(tokens, output, keyval, sent, bound, held, sems):
    count, half, width = sent.shape
    head = output.shape[0]
    start = pl.multiple_of(own_core() * half, half)
    copies = [
        pltpu.make_async_copy(output, held.at[pl.ds(0, head), :], sems.at[1, 0]),
        pltpu.make_async_copy(keyval, held.at[pl.ds(head, keyval.shape[0]), :], sems.at[1, 1]),
    ]
    for q in range(count):
        source = tokens.at[pl.ds(start, half), pl.ds(q * width, width)]
        copies.append(pltpu.make_async_copy(source, sent.at[q], sems.at[0, q]))
    for copy in copies:
        copy.start()
    for copy in copies[:2]:
        copy.wait()
    save = pltpu.make_async_copy(held, bound, sems.at[1, 2])
    save.start()
    for copy in copies[2:]:
        copy.wait()
    save.wait()


def cut(tokens, output, keyval, count):
    rows, depth = tokens.shape
    together = (output.shape[0] + keyval.shape[0], output.shape[1])
    outs = [bfloat(count, rows // 2, depth // count), bfloat(*together)]
    scratch = [pltpu.VMEM(together, jnp.bfloat16), pltpu.SemaphoreType.DMA((2, max(3, count)))]
    return call(cut_kernel, "cut", outs, [HBM] * 3, [tokens, output, keyval], scratch, [VMEM, HBM])


def widen_kernel(query, keyval, wide, tall):
    head, piece = query.shape[1], keyval.shape[0]
    wide[:, :head] = query[...]
    tall[:piece, :] = keyval[...]
    tall[piece:, :] = jnp.zeros((LANES - piece, tall.shape[1]), tall.dtype)
    for low in range(0, query.shape[0], LANES):
        block = tall[:, low : low + LANES].astype(jnp.float32)
        wide[low : low + LANES, head:] = jnp.transpose(block).astype(jnp.bfloat16)


def widen(query, keyval):
    depth, head = query.shape
    scratch = [pltpu.VMEM((LANES, depth), jnp.bfloat16)]
    outs = [bfloat(depth, head + LANES)]
    return call(widen_kernel, "widen", outs, [VMEM] * 2, [query, keyval], scratch)[0]


def norm_kernel(tokens, scale, whole, sems):
    pieces = sems.shape[0]
    step = tokens.shape[1] // pieces
    copies = []
    for p in range(pieces):
        columns = pl.ds(p * step, step)
        copies.append(pltpu.make_async_copy(tokens.at[:, columns], whole.at[:, columns], sems.at[p]))
    for copy in copies:
        copy.start()
    total = jnp.zeros((tokens.shape[0], LANES), jnp.float32)
    for p, copy in enumerate(copies):
        copy.wait()
        for low in range(p * step, (p + 1) * step, LANES):
            floats = whole[:, low : low + LANES].astype(jnp.float32)
            total = total + floats * floats
    squares = jnp.sum(total, axis=1, keepdims=True)
    scale[...] = lax.rsqrt(squares / tokens.shape[1] + EPS)


def norms(tokens):
    outs = [jax.ShapeDtypeStruct((tokens.shape[0], 1), jnp.float32)]
    scratch = [pltpu.VMEM(tokens.shape, jnp.bfloat16), pltpu.SemaphoreType.DMA((4,))]
    return call(norm_kernel, "norms", outs, [HBM], [tokens], scratch)[0]


def slice_kernel(shard, queries, *pieces):
    count = len(pieces)
    sub = pieces[0].shape[0]
    for i in range(count):

        @pl.when(lax.axis_index("inst") == i)
        def give():
            for d, piece in enumerate(pieces):
                low = (i + d) % count * sub
                piece[...] = shard[low : low + sub, :]


def slices(shard, queries, count):
    head, width = shard.shape
    return call(slice_kernel, "slices", [bfloat(head // count, width)] * count, [VMEM] * 2, [shard, queries])


def aim_kernel(count, *refs):
    arrived, pieces, held = refs[:count], refs[count:-1], refs[-1]
    for d, block in enumerate(arrived):
        held[lax.rem(lax.axis_index("inst") - d + count, count)] = block[...]
    for e, piece in enumerate(pieces):
        piece[...] = held[lax.rem(lax.axis_index("tp") // 2 + e, len(pieces))]


def aim(arrived, planes):
    shape = arrived[0].shape
    kernel = functools.partial(aim_kernel, len(arrived))
    scratch = [pltpu.VMEM((len(arrived), *shape), jnp.bfloat16)]
    return call(kernel, "aim", [bfloat(*shape)] * planes, [VMEM] * len(arrived), arrived, scratch)


def keep_kernel(source, output, *refs):
    pieces, (kept, rows) = refs[:-2], refs[-2:]
    kept[...] = source[...]
    for e, piece in enumerate(pieces):
        rows[e] = piece[...]


def keep(block, output, pieces):
    outs = [bfloat(*block.shape), bfloat(len(pieces), *pieces[0].shape)]
    ins = [VMEM, HBM] + [VMEM] * len(pieces)
    return call(keep_kernel, "keep", outs, ins, [block, output, *pieces], places=[VMEM, LAST])


def project_kernel(rows, weight, *refs):
    first, (saved, sums, sem) = refs[:-3], refs[-3:]
    count, half, width = rows.shape
    save = pltpu.make_async_copy(rows, saved, sem)
    save.start()
    hidden = rows[...].reshape(count * half, width)
    total = jnp.dot(hidden, weight[...], preferred_element_type=jnp.float32).astype(jnp.bfloat16)
    core = own_core()
    for q in range(count):
        block = total[q * half : (q + 1) * half]
        if first:
            sums[q, pl.ds(pl.multiple_of(core * half, half), half), :] = first[0][q]
            sums[q, pl.ds(pl.multiple_of((1 - core) * half, half), half), :] = block
        else:
            sums[q] = block
    save.wait()


def project(rows, weight, *first):
    count, half, width = rows.shape
    outs = [bfloat(*rows.shape), bfloat(count, half * (1 + len(first)), weight.shape[1])]
    args = [rows, weight, *first]
    scratch = [pltpu.SemaphoreType.DMA(())]
    return call(project_kernel, "project", outs, [VMEM] * len(args), args, scratch, [HBM, VMEM])


def summed(parts):
    total = parts[0].astype(jnp.float32)
    for part in parts[1:]:
        total = total + part.astype(jnp.float32)
    return total


def finish_kernel(parts, scale, queries, keyvals_t):
    head = queries.shape[1]
    total = summed([parts[q] for q in range(parts.shape[0])]) * scale[...]
    queries[...] = (total[:, :head] * head ** (-0.5)).astype(jnp.bfloat16)
    piece = transposed(total[:, head:].astype(jnp.bfloat16), keyvals_t.shape[1])
    for g in range(keyvals_t.shape[0]):
        keyvals_t[g] = piece


def finish(parts, scale, head, piece):
    rows = parts.shape[1]
    outs = [bfloat(rows, head), bfloat(GROUP, piece, rows)]
    return call(finish_kernel, "finish", outs, [VMEM] * 2, [parts, scale])


def attention(queries, keys_t, values_t, dims, doc_ids, back):
    rows = queries.shape[0]
    at = lax.broadcasted_iota(jnp.int32, (rows, rows), 0)
    key_at = lax.broadcasted_iota(jnp.int32, (rows, rows), 1)
    count = doc_ids.shape[0]
    own = lax.rem(lax.axis_index("inst") - back + count, count)
    docs_row = jnp.broadcast_to(doc_ids[pl.ds(own, 1), :].astype(jnp.float32), (rows, rows))
    docs_column = jnp.sum(jnp.where(at == key_at, docs_row, 0.0), axis=1, keepdims=True)
    allowed = (docs_column == docs_row) & (key_at <= at)
    scores = contract(queries, keys_t, (1, dims[0]))
    scores = jnp.where(allowed, scores, -1e30)
    weights = jnp.exp(scores - jnp.max(scores, axis=1, keepdims=True))
    probabilities = weights / jnp.sum(weights, axis=1, keepdims=True)
    return contract(probabilities.astype(jnp.bfloat16), values_t, (1, dims[1])).astype(jnp.bfloat16)


def first_kernel(queries, doc_ids, pieces, *refs):
    context = refs[-1]
    span = pieces.shape[0] // 2
    keys_t = jnp.concatenate([pieces[g] for g in range(span)], 0)
    values_t = jnp.concatenate([pieces[g] for g in range(span, 2 * span)], 0)
    result = attention(queries[...], keys_t, values_t, (0, 1), doc_ids, 0)
    for z in range(context.shape[0]):
        context[z] = result


def first_attend(queries, doc_ids, pieces, arrived):
    outs = [bfloat(lax.axis_size("tp") // 2, *queries.shape)]
    args = [queries, doc_ids, pieces, *arrived]
    return call(first_kernel, "attend", outs, [VMEM] * len(args), args)[0]


def second_kernel(depth, head, rows, parts, doc_ids, sent):
    wide = 3 * head
    total = summed([parts[q, :rows, :wide] for q in range(parts.shape[0])])
    high = summed([parts[q, rows : rows + 16, :] for q in range(parts.shape[0])])
    across = jnp.broadcast_to(high[0:1] + high[1:2], (rows, parts.shape[2]))
    at = lax.broadcasted_iota(jnp.int32, across.shape, 0)
    lane = lax.broadcasted_iota(jnp.int32, across.shape, 1)
    squares = jnp.sum(jnp.where(at == lane, across, 0.0), axis=1, keepdims=True)
    total = total * lax.rsqrt(squares / depth + EPS)
    queries = (total[:, :head] * head ** (-0.5)).astype(jnp.bfloat16)
    keys = total[:, head : 2 * head].astype(jnp.bfloat16)
    values = total[:, 2 * head :].astype(jnp.bfloat16)
    result = attention(queries, keys, values, (1, 0), doc_ids, 1)
    for z in range(sent.shape[0]):
        sent[z, :, :head] = result
        sent[z, :, head:] = parts[z, :rows, wide:]


def second_attend(parts, doc_ids, depth, head):
    rows = doc_ids.shape[1]
    outs = [bfloat(parts.shape[0], rows, parts.shape[2] - 2 * head)]
    kernel = functools.partial(second_kernel, depth, head, rows)
    return call(kernel, "attend", outs, [VMEM] * 2, [parts, doc_ids])[0]


def spread_kernel(heads, sent):
    for q in range(sent.shape[0]):
        sent[q] = heads[...]


def spread(heads):
    outs = [bfloat(lax.axis_size("inst"), *heads.shape)]
    return call(spread_kernel, "spread", outs, [VMEM], [heads])[0]


def spans(count):
    return [range(low, min(low + 4, count)) for low in range(0, count, 4)]


def place_contexts(mine, other, left, span):
    _, pairs, rows, head = mine.shape
    core = own_core()
    for source, parity in ((mine, core), (other, 1 - core)):
        for e in range(pairs):
            columns = pl.ds(pl.multiple_of((2 * e + parity) * head, head), head)
            for at, q in enumerate(span):
                left[at * rows : (at + 1) * rows, columns] = source[q, e]


def advance_kernel(step, own_rows, other_rows, mine, other, output, query, rows_by, sums, left, held, tall, hidden, blended, sems):
    count, pairs, rows, head = mine.shape
    width = own_rows.shape[2]
    ranks = 2 * pairs
    core = own_core()
    first = lax.axis_index("tp") // GROUP * GROUP
    copies = []
    for at in range(width // step):
        columns = pl.ds(at * step, step)
        pairs_of = [
            (output.at[:, pl.ds(0, head), columns], held.at[:, :, columns]),
            (own_rows.at[:, :, columns], hidden.at[:, core, :, columns]),
            (other_rows.at[:, :, columns], hidden.at[:, 1 - core, :, columns]),
            (output.at[pl.ds(first, GROUP), pl.ds(head, tall.shape[1]), columns], tall.at[:, :, columns]),
        ]
        copies.append([pltpu.make_async_copy(*pair, sems.at[c, at]) for c, pair in enumerate(pairs_of)])
    for chunk in copies:
        for copy in chunk:
            copy.start()
    for span in spans(count):
        place_contexts(mine, other, left, span)
        low, high = span[0] * rows, (span[-1] + 1) * rows
        queries, keyvals, squares = 0.0, 0.0, jnp.zeros((high - low, LANES), jnp.float32)
        for at, chunk in enumerate(copies):
            if span[0] == 0:
                for copy in chunk:
                    copy.wait()
            columns = pl.ds(at * step, step)
            right = held[:, :, columns].reshape(ranks * head, step)
            attended = jnp.dot(left[: high - low, :], right, preferred_element_type=jnp.float32)
            before = hidden[span[0] : span[-1] + 1, :, :, columns].reshape(high - low, step)
            after_one = (before.astype(jnp.float32) + attended).astype(jnp.bfloat16)
            blended[low:high, columns] = after_one
            queries = queries + jnp.dot(after_one, query[columns, :], preferred_element_type=jnp.float32)
            right = tall[:, :, columns].reshape(GROUP * tall.shape[1], step)
            keyvals = keyvals + contract(after_one, right, (1, 1))
            floats = after_one.astype(jnp.float32)
            for lane in range(0, step, LANES):
                part = floats[:, lane : lane + LANES]
                squares = squares + part * part
        squares = jnp.sum(squares, axis=1, keepdims=True)
        queries, keyvals = queries.astype(jnp.bfloat16), keyvals.astype(jnp.bfloat16)
        for at, q in enumerate(span):
            slot = (q + 1) % count
            block = slice(at * rows, (at + 1) * rows)
            sums[slot, :rows, :head] = queries[block]
            sums[slot, :rows, head : 3 * head] = keyvals[block]
            lanes = sums.shape[2]
            row = lax.broadcasted_iota(jnp.int32, (rows, lanes), 0)
            lane = lax.broadcasted_iota(jnp.int32, (rows, lanes), 1)
            square = jnp.where(row == lane, squares[block], 0.0)
            square = jnp.sum(square, axis=0, keepdims=True)
            high_part = square.astype(jnp.bfloat16).astype(jnp.float32)
            row = lax.broadcasted_iota(jnp.int32, (16, lanes), 0)
            extra = jnp.where(row == 0, high_part, jnp.where(row == 1, square - high_part, 0.0))
            sums[slot, rows:, :] = extra.astype(jnp.bfloat16)
    wide = 3 * head
    slim = (sums.shape[2] - wide) // 2
    for r in range(ranks):

        @pl.when(lax.axis_index("tp") == r)
        def give():
            for b in range(2):
                low = b * (width // 2) + r * slim
                for q in range(count):
                    block = blended[q * rows : (q + 1) * rows, low : low + slim]
                    sums[(q + 1) % count, :rows, wide + b * slim : wide + (b + 1) * slim] = block


def advance(own_rows, other_rows, mine, other, output, query, rows_by):
    count, pairs, rows, head = mine.shape
    width = own_rows.shape[2]
    total = count * rows
    step = min(512, width)
    ranks, both, _ = output.shape
    scratch = [
        pltpu.VMEM((min(4, count) * rows, ranks * head), jnp.bfloat16),
        pltpu.VMEM((ranks, head, width), jnp.bfloat16),
        pltpu.VMEM((GROUP, both - head, width), jnp.bfloat16),
        pltpu.VMEM((count, 2, rows // 2, width), jnp.bfloat16),
        pltpu.VMEM((total, width), jnp.bfloat16),
        pltpu.SemaphoreType.DMA((4, width // step)),
    ]
    outs = [bfloat(count, rows + 16, 3 * head + width // ranks)]
    ins = [HBM] * 2 + [VMEM] * 2 + [HBM, VMEM, HBM]
    args = [own_rows, other_rows, mine, other, output, query, rows_by]
    return call(functools.partial(advance_kernel, step), "advance", outs, ins, args, scratch)[0]


def blend_kernel(swap, got, rows_by, out, held, sems):
    pairs, rows, _ = got.shape
    count, _, sub, _ = rows_by.shape
    head = count * sub
    plane = lax.axis_index("tp") // 2
    half = out.shape[1]
    slim = half // (2 * pairs)
    core = own_core()
    place = 1 - core if swap else core
    copies = []
    for i in range(count):
        for e in range(pairs):
            source = rows_by.at[i, e, :, pl.ds(pl.multiple_of(place * half, half), half)]
            target = held.at[pl.ds(e * head + i * sub, sub), :]
            copies.append(pltpu.make_async_copy(source, target, sems.at[i, e]))
    for copy in copies:
        copy.start()
    left = jnp.concatenate([got[lax.rem(plane - e + pairs, pairs), :, :head] for e in range(pairs)], 1)
    rest = []
    for a in range(pairs):
        low = got[a, :, head : head + slim]
        high = got[a, :, head + slim : head + 2 * slim]
        ours = jnp.where(place == 0, low, high).astype(jnp.float32)
        rest += [jnp.where(core == 0, ours, 0.0), jnp.where(core == 0, 0.0, ours)]
    rest = jnp.concatenate(rest, 1)
    for copy in copies:
        copy.wait()
    total = jnp.dot(left, held[...], preferred_element_type=jnp.float32) + rest
    out[...] = total.astype(out.dtype)


def blend(got, rows_by, swap):
    pairs, rows, _ = got.shape
    count, _, sub, width = rows_by.shape
    scratch = [pltpu.VMEM((pairs * count * sub, width // 2), jnp.bfloat16), pltpu.SemaphoreType.DMA((count, pairs))]
    outs = [jax.ShapeDtypeStruct((rows, width // 2), jnp.bfloat16 if swap else jnp.float32)]
    kernel = functools.partial(blend_kernel, swap)
    return call(kernel, "blend", outs, [VMEM, HBM], [got, rows_by], scratch)[0]


def join_kernel(kept, arrived, blended):
    blended[...] = (kept[...] + arrived[...].astype(jnp.float32)).astype(jnp.bfloat16)


def join(kept, arrived):
    return call(join_kernel, "join", [bfloat(*kept.shape)], [VMEM] * 2, [kept, arrived], places=[LAST])[0]


def shards(tokens, doc_ids, query_one, keyval_one, output_one, query_two, keyval_two, output_two):
    count, ranks = lax.axis_size("inst"), lax.axis_size("tp")
    rows, depth = tokens.shape
    head, piece = query_one.shape[1], keyval_one.shape[1]
    groups = None
    if ranks > GROUP:
        groups = [list(range(low, low + GROUP)) for low in range(0, ranks, GROUP)]

    sent, bound = cut(tokens, output_one, keyval_two.T, count)
    output_all = lax.all_gather(bound, "tp", axis=0)
    mine = exchange(sent, "inst")
    weight = widen(query_one, keyval_one.T)
    own_rows, first = project(mine, weight)
    other_rows, sums = project(other_core(mine), weight, first)
    queries, keyvals_t = finish(exchange(sums, "inst"), norms(tokens), head, piece)
    arrived = slices(output_two, queries, count)
    arrived = [arrived[0]] + [shifted(arrived[d], "inst", d) for d in range(1, count)]
    pieces = aim(arrived, ranks // 2)
    pieces = [pieces[0]] + [shifted(pieces[e], "tp", 2 * e) for e in range(1, ranks // 2)]
    context = first_attend(queries, doc_ids, exchange(keyvals_t, "tp", groups), arrived)
    heads = exchange(context, "tp", core_groups())
    mine, rows_by = keep(exchange(spread(heads), "inst"), output_all, pieces)
    sums = advance(own_rows, other_rows, mine, other_core(mine), output_all, query_two, rows_by)
    rows_by = lax.all_gather(rows_by, "inst", axis=0)

    sent = second_attend(exchange(sums, "inst"), doc_ids, depth, head)
    got = exchange(sent, "tp", core_groups())
    arrived = other_core(blend(got, rows_by, True))
    return join(blend(got, rows_by, False), arrived)


def solution(mesh):
    placed = (
        P("inst", None),
        P(),
        P("inst", "tp"),
        P("inst", "tp"),
        P("tp", "inst"),
        P("inst", "tp"),
        P("inst", "tp"),
        P("tp", "inst"),
    )
    return jax.shard_map(
        shards, mesh=mesh, in_specs=placed, out_specs=P("inst", "tp"), check_vma=False
    )
```

```python
import functools
import math

import jax
import jax.numpy as jnp
from jax import lax
from jax.experimental import pallas as pl
from jax.experimental.pallas import tpu as pltpu
from jax.sharding import PartitionSpec as P

GROUP = 8
EPS = 1e-6
LANES = 128
VMEM = pl.BlockSpec(memory_space=pltpu.VMEM)
HBM = pl.BlockSpec(memory_space=pltpu.MemorySpace.HBM)
LAST = pl.BlockSpec(memory_space=pltpu.VMEM)


def contract(left, right, dims):
    return lax.dot_general(left, right, ((dims[:1], dims[1:]), ((), ())), preferred_element_type=jnp.float32)


def exchange(block, axis, groups=None):
    return lax.all_to_all(block, axis, 0, 0, axis_index_groups=groups)


def other_core(block):
    count = lax.axis_size("tp")
    return lax.ppermute(block, "tp", [(s, s ^ 1) for s in range(count)])


def own_core():
    return lax.rem(lax.axis_index("tp"), 2)


def transposed(block, rows):
    row = lax.broadcasted_iota(jnp.int32, (rows, block.shape[1]), 0)
    column = lax.broadcasted_iota(jnp.int32, (rows, block.shape[1]), 1)
    pick = (row == column).astype(jnp.bfloat16)
    return contract(pick, block, (1, 1)).astype(jnp.bfloat16)


def call(kernel, name, outs, ins, args, scratch=(), places=None):
    places = places or [VMEM] * len(outs)
    held = [value for value, spec in zip([*args, *outs], [*ins, *places]) if spec is VMEM]
    total = sum(math.prod(value.shape) * value.dtype.itemsize for value in held)
    work = sum(math.prod(ref.shape) * ref.dtype.itemsize for ref in scratch if hasattr(ref.dtype, "itemsize"))
    resident = total <= 16 * 2**20
    if resident:
        spaces = [spec.memory_space for spec in ins]
        args = [pltpu.with_memory_space_constraint(value, space) for value, space in zip(args, spaces)]
        outs = [out if spec is LAST else spec.memory_space(out.shape, out.dtype) for out, spec in zip(outs, places)]
        limit = work + 12 * 2**20
    else:
        limit = 56 * 2**20
    return pl.pallas_call(
        kernel,
        out_shape=outs,
        in_specs=ins,
        out_specs=[VMEM if spec is LAST else spec for spec in places],
        scratch_shapes=list(scratch),
        compiler_params=pltpu.CompilerParams(vmem_limit_bytes=limit),
        name=name,
    )(*args)


def bfloat(*shape):
    return jax.ShapeDtypeStruct(shape, jnp.bfloat16)


def shifted(block, axis, distance):
    count = lax.axis_size(axis)
    return lax.ppermute(block, axis, [(s, (s + distance) % count) for s in range(count)])


def core_groups():
    ranks = lax.axis_size("tp")
    return [list(range(core, ranks, 2)) for core in range(2)]


def cut_kernel(tokens, output, keyval, sent, bound, held, sems):
    count, half, width = sent.shape
    head = output.shape[0]
    start = pl.multiple_of(own_core() * half, half)
    copies = [
        pltpu.make_async_copy(output, held.at[pl.ds(0, head), :], sems.at[1, 0]),
        pltpu.make_async_copy(keyval, held.at[pl.ds(head, keyval.shape[0]), :], sems.at[1, 1]),
    ]
    for q in range(count):
        source = tokens.at[pl.ds(start, half), pl.ds(q * width, width)]
        copies.append(pltpu.make_async_copy(source, sent.at[q], sems.at[0, q]))
    for copy in copies:
        copy.start()
    for copy in copies[:2]:
        copy.wait()
    save = pltpu.make_async_copy(held, bound, sems.at[1, 2])
    save.start()
    for copy in copies[2:]:
        copy.wait()
    save.wait()


def cut(tokens, output, keyval, count):
    rows, depth = tokens.shape
    together = (output.shape[0] + keyval.shape[0], output.shape[1])
    outs = [bfloat(count, rows // 2, depth // count), bfloat(*together)]
    scratch = [pltpu.VMEM(together, jnp.bfloat16), pltpu.SemaphoreType.DMA((2, max(3, count)))]
    return call(cut_kernel, "cut", outs, [HBM] * 3, [tokens, output, keyval], scratch, [VMEM, HBM])


def widen_kernel(query, keyval, wide, tall):
    head, piece = query.shape[1], keyval.shape[0]
    wide[:, :head] = query[...]
    tall[:piece, :] = keyval[...]
    tall[piece:, :] = jnp.zeros((LANES - piece, tall.shape[1]), tall.dtype)
    for low in range(0, query.shape[0], LANES):
        block = tall[:, low : low + LANES].astype(jnp.float32)
        wide[low : low + LANES, head:] = jnp.transpose(block).astype(jnp.bfloat16)


def widen(query, keyval):
    depth, head = query.shape
    scratch = [pltpu.VMEM((LANES, depth), jnp.bfloat16)]
    outs = [bfloat(depth, head + LANES)]
    return call(widen_kernel, "widen", outs, [VMEM] * 2, [query, keyval], scratch)[0]


def norm_kernel(tokens, scale, whole, sems):
    pieces = sems.shape[0]
    step = tokens.shape[1] // pieces
    copies = []
    for p in range(pieces):
        columns = pl.ds(p * step, step)
        copies.append(pltpu.make_async_copy(tokens.at[:, columns], whole.at[:, columns], sems.at[p]))
    for copy in copies:
        copy.start()
    total = jnp.zeros((tokens.shape[0], LANES), jnp.float32)
    for p, copy in enumerate(copies):
        copy.wait()
        for low in range(p * step, (p + 1) * step, LANES):
            floats = whole[:, low : low + LANES].astype(jnp.float32)
            total = total + floats * floats
    squares = jnp.sum(total, axis=1, keepdims=True)
    scale[...] = lax.rsqrt(squares / tokens.shape[1] + EPS)


def norms(tokens):
    outs = [jax.ShapeDtypeStruct((tokens.shape[0], 1), jnp.float32)]
    scratch = [pltpu.VMEM(tokens.shape, jnp.bfloat16), pltpu.SemaphoreType.DMA((4,))]
    return call(norm_kernel, "norms", outs, [HBM], [tokens], scratch)[0]


def slice_kernel(shard, queries, *pieces):
    count = len(pieces)
    sub = pieces[0].shape[0]
    for i in range(count):

        @pl.when(lax.axis_index("inst") == i)
        def give():
            for d, piece in enumerate(pieces):
                low = (i + d) % count * sub
                piece[...] = shard[low : low + sub, :]


def slices(shard, queries, count):
    head, width = shard.shape
    return call(slice_kernel, "slices", [bfloat(head // count, width)] * count, [VMEM] * 2, [shard, queries])


def aim_kernel(count, *refs):
    arrived, pieces, held = refs[:count], refs[count:-1], refs[-1]
    for d, block in enumerate(arrived):
        held[lax.rem(lax.axis_index("inst") - d + count, count)] = block[...]
    for e, piece in enumerate(pieces):
        piece[...] = held[lax.rem(lax.axis_index("tp") // 2 + e, len(pieces))]


def aim(arrived, planes):
    shape = arrived[0].shape
    kernel = functools.partial(aim_kernel, len(arrived))
    scratch = [pltpu.VMEM((len(arrived), *shape), jnp.bfloat16)]
    return call(kernel, "aim", [bfloat(*shape)] * planes, [VMEM] * len(arrived), arrived, scratch)


def keep_kernel(source, output, *refs):
    pieces, (kept, rows) = refs[:-2], refs[-2:]
    kept[...] = source[...]
    for e, piece in enumerate(pieces):
        rows[e] = piece[...]


def keep(block, output, pieces):
    outs = [bfloat(*block.shape), bfloat(len(pieces), *pieces[0].shape)]
    ins = [VMEM, HBM] + [VMEM] * len(pieces)
    return call(keep_kernel, "keep", outs, ins, [block, output, *pieces], places=[VMEM, LAST])


def project_kernel(rows, weight, *refs):
    first, (saved, sums, sem) = refs[:-3], refs[-3:]
    count, half, width = rows.shape
    save = pltpu.make_async_copy(rows, saved, sem)
    save.start()
    hidden = rows[...].reshape(count * half, width)
    total = jnp.dot(hidden, weight[...], preferred_element_type=jnp.float32).astype(jnp.bfloat16)
    core = own_core()
    for q in range(count):
        block = total[q * half : (q + 1) * half]
        if first:
            sums[q, pl.ds(pl.multiple_of(core * half, half), half), :] = first[0][q]
            sums[q, pl.ds(pl.multiple_of((1 - core) * half, half), half), :] = block
        else:
            sums[q] = block
    save.wait()


def project(rows, weight, *first):
    count, half, width = rows.shape
    outs = [bfloat(*rows.shape), bfloat(count, half * (1 + len(first)), weight.shape[1])]
    args = [rows, weight, *first]
    scratch = [pltpu.SemaphoreType.DMA(())]
    return call(project_kernel, "project", outs, [VMEM] * len(args), args, scratch, [HBM, VMEM])


def summed(parts):
    total = parts[0].astype(jnp.float32)
    for part in parts[1:]:
        total = total + part.astype(jnp.float32)
    return total


def finish_kernel(parts, scale, queries, keyvals_t):
    head = queries.shape[1]
    total = summed([parts[q] for q in range(parts.shape[0])]) * scale[...]
    queries[...] = (total[:, :head] * head ** (-0.5)).astype(jnp.bfloat16)
    piece = transposed(total[:, head:].astype(jnp.bfloat16), keyvals_t.shape[1])
    for g in range(keyvals_t.shape[0]):
        keyvals_t[g] = piece


def finish(parts, scale, head, piece):
    rows = parts.shape[1]
    outs = [bfloat(rows, head), bfloat(GROUP, piece, rows)]
    return call(finish_kernel, "finish", outs, [VMEM] * 2, [parts, scale])


def attention(queries, keys_t, values_t, dims, doc_ids, back):
    rows = queries.shape[0]
    at = lax.broadcasted_iota(jnp.int32, (rows, rows), 0)
    key_at = lax.broadcasted_iota(jnp.int32, (rows, rows), 1)
    count = doc_ids.shape[0]
    own = lax.rem(lax.axis_index("inst") - back + count, count)
    docs_row = jnp.broadcast_to(doc_ids[pl.ds(own, 1), :].astype(jnp.float32), (rows, rows))
    docs_column = jnp.sum(jnp.where(at == key_at, docs_row, 0.0), axis=1, keepdims=True)
    allowed = (docs_column == docs_row) & (key_at <= at)
    scores = contract(queries, keys_t, (1, dims[0]))
    scores = jnp.where(allowed, scores, -1e30)
    weights = jnp.exp(scores - jnp.max(scores, axis=1, keepdims=True))
    probabilities = weights / jnp.sum(weights, axis=1, keepdims=True)
    return contract(probabilities.astype(jnp.bfloat16), values_t, (1, dims[1])).astype(jnp.bfloat16)


def first_kernel(queries, doc_ids, pieces, *refs):
    context = refs[-1]
    span = pieces.shape[0] // 2
    keys_t = jnp.concatenate([pieces[g] for g in range(span)], 0)
    values_t = jnp.concatenate([pieces[g] for g in range(span, 2 * span)], 0)
    result = attention(queries[...], keys_t, values_t, (0, 1), doc_ids, 0)
    for z in range(context.shape[0]):
        context[z] = result


def first_attend(queries, doc_ids, pieces, arrived):
    outs = [bfloat(lax.axis_size("tp") // 2, *queries.shape)]
    args = [queries, doc_ids, pieces, *arrived]
    return call(first_kernel, "attend", outs, [VMEM] * len(args), args)[0]


def second_kernel(depth, head, rows, parts, doc_ids, sent):
    wide = 3 * head
    total = summed([parts[q, :rows, :wide] for q in range(parts.shape[0])])
    high = summed([parts[q, rows : rows + 16, :] for q in range(parts.shape[0])])
    across = jnp.broadcast_to(high[0:1] + high[1:2], (rows, parts.shape[2]))
    at = lax.broadcasted_iota(jnp.int32, across.shape, 0)
    lane = lax.broadcasted_iota(jnp.int32, across.shape, 1)
    squares = jnp.sum(jnp.where(at == lane, across, 0.0), axis=1, keepdims=True)
    total = total * lax.rsqrt(squares / depth + EPS)
    queries = (total[:, :head] * head ** (-0.5)).astype(jnp.bfloat16)
    keys = total[:, head : 2 * head].astype(jnp.bfloat16)
    values = total[:, 2 * head :].astype(jnp.bfloat16)
    result = attention(queries, keys, values, (1, 0), doc_ids, 1)
    for z in range(sent.shape[0]):
        sent[z, :, :head] = result
        sent[z, :, head:] = parts[z, :rows, wide:]


def second_attend(parts, doc_ids, depth, head):
    rows = doc_ids.shape[1]
    outs = [bfloat(parts.shape[0], rows, parts.shape[2] - 2 * head)]
    kernel = functools.partial(second_kernel, depth, head, rows)
    return call(kernel, "attend", outs, [VMEM] * 2, [parts, doc_ids])[0]


def spread_kernel(heads, sent):
    for q in range(sent.shape[0]):
        sent[q] = heads[...]


def spread(heads):
    outs = [bfloat(lax.axis_size("inst"), *heads.shape)]
    return call(spread_kernel, "spread", outs, [VMEM], [heads])[0]


def spans(count):
    return [range(low, min(low + 4, count)) for low in range(0, count, 4)]


def place_contexts(mine, other, left, span):
    _, pairs, rows, head = mine.shape
    core = own_core()
    for source, parity in ((mine, core), (other, 1 - core)):
        for e in range(pairs):
            columns = pl.ds(pl.multiple_of((2 * e + parity) * head, head), head)
            for at, q in enumerate(span):
                left[at * rows : (at + 1) * rows, columns] = source[q, e]


def advance_kernel(step, own_rows, other_rows, mine, other, output, query, rows_by, sums, left, held, tall, hidden, blended, sems):
    count, pairs, rows, head = mine.shape
    width = own_rows.shape[2]
    ranks = 2 * pairs
    core = own_core()
    first = lax.axis_index("tp") // GROUP * GROUP
    copies = []
    for at in range(width // step):
        columns = pl.ds(at * step, step)
        pairs_of = [
            (output.at[:, pl.ds(0, head), columns], held.at[:, :, columns]),
            (own_rows.at[:, :, columns], hidden.at[:, core, :, columns]),
            (other_rows.at[:, :, columns], hidden.at[:, 1 - core, :, columns]),
            (output.at[pl.ds(first, GROUP), pl.ds(head, tall.shape[1]), columns], tall.at[:, :, columns]),
        ]
        copies.append([pltpu.make_async_copy(*pair, sems.at[c, at]) for c, pair in enumerate(pairs_of)])
    for chunk in copies:
        for copy in chunk:
            copy.start()
    for span in spans(count):
        place_contexts(mine, other, left, span)
        low, high = span[0] * rows, (span[-1] + 1) * rows
        queries, keyvals, squares = 0.0, 0.0, jnp.zeros((high - low, LANES), jnp.float32)
        for at, chunk in enumerate(copies):
            if span[0] == 0:
                for copy in chunk:
                    copy.wait()
            columns = pl.ds(at * step, step)
            right = held[:, :, columns].reshape(ranks * head, step)
            attended = jnp.dot(left[: high - low, :], right, preferred_element_type=jnp.float32)
            before = hidden[span[0] : span[-1] + 1, :, :, columns].reshape(high - low, step)
            after_one = (before.astype(jnp.float32) + attended).astype(jnp.bfloat16)
            blended[low:high, columns] = after_one
            queries = queries + jnp.dot(after_one, query[columns, :], preferred_element_type=jnp.float32)
            right = tall[:, :, columns].reshape(GROUP * tall.shape[1], step)
            keyvals = keyvals + contract(after_one, right, (1, 1))
            floats = after_one.astype(jnp.float32)
            for lane in range(0, step, LANES):
                part = floats[:, lane : lane + LANES]
                squares = squares + part * part
        squares = jnp.sum(squares, axis=1, keepdims=True)
        queries, keyvals = queries.astype(jnp.bfloat16), keyvals.astype(jnp.bfloat16)
        for at, q in enumerate(span):
            slot = (q + 1) % count
            block = slice(at * rows, (at + 1) * rows)
            sums[slot, :rows, :head] = queries[block]
            sums[slot, :rows, head : 3 * head] = keyvals[block]
            lanes = sums.shape[2]
            row = lax.broadcasted_iota(jnp.int32, (rows, lanes), 0)
            lane = lax.broadcasted_iota(jnp.int32, (rows, lanes), 1)
            square = jnp.where(row == lane, squares[block], 0.0)
            square = jnp.sum(square, axis=0, keepdims=True)
            high_part = square.astype(jnp.bfloat16).astype(jnp.float32)
            row = lax.broadcasted_iota(jnp.int32, (16, lanes), 0)
            extra = jnp.where(row == 0, high_part, jnp.where(row == 1, square - high_part, 0.0))
            sums[slot, rows:, :] = extra.astype(jnp.bfloat16)
    wide = 3 * head
    slim = (sums.shape[2] - wide) // 2
    for r in range(ranks):

        @pl.when(lax.axis_index("tp") == r)
        def give():
            for b in range(2):
                low = b * (width // 2) + r * slim
                for q in range(count):
                    block = blended[q * rows : (q + 1) * rows, low : low + slim]
                    sums[(q + 1) % count, :rows, wide + b * slim : wide + (b + 1) * slim] = block


def advance(own_rows, other_rows, mine, other, output, query, rows_by):
    count, pairs, rows, head = mine.shape
    width = own_rows.shape[2]
    total = count * rows
    step = min(1024, width)
    ranks, both, _ = output.shape
    scratch = [
        pltpu.VMEM((min(4, count) * rows, ranks * head), jnp.bfloat16),
        pltpu.VMEM((ranks, head, width), jnp.bfloat16),
        pltpu.VMEM((GROUP, both - head, width), jnp.bfloat16),
        pltpu.VMEM((count, 2, rows // 2, width), jnp.bfloat16),
        pltpu.VMEM((total, width), jnp.bfloat16),
        pltpu.SemaphoreType.DMA((4, width // step)),
    ]
    outs = [bfloat(count, rows + 16, 3 * head + width // ranks)]
    ins = [HBM] * 2 + [VMEM] * 2 + [HBM, VMEM, HBM]
    args = [own_rows, other_rows, mine, other, output, query, rows_by]
    return call(functools.partial(advance_kernel, step), "advance", outs, ins, args, scratch)[0]


def blend_kernel(swap, got, rows_by, out, held, sems):
    pairs, rows, _ = got.shape
    count, _, sub, _ = rows_by.shape
    head = count * sub
    plane = lax.axis_index("tp") // 2
    half = out.shape[1]
    slim = half // (2 * pairs)
    core = own_core()
    place = 1 - core if swap else core
    copies = []
    for i in range(count):
        for e in range(pairs):
            source = rows_by.at[i, e, :, pl.ds(pl.multiple_of(place * half, half), half)]
            target = held.at[pl.ds(e * head + i * sub, sub), :]
            copies.append(pltpu.make_async_copy(source, target, sems.at[i, e]))
    for copy in copies:
        copy.start()
    left = jnp.concatenate([got[lax.rem(plane - e + pairs, pairs), :, :head] for e in range(pairs)], 1)
    rest = []
    for a in range(pairs):
        low = got[a, :, head : head + slim]
        high = got[a, :, head + slim : head + 2 * slim]
        ours = jnp.where(place == 0, low, high).astype(jnp.float32)
        rest += [jnp.where(core == 0, ours, 0.0), jnp.where(core == 0, 0.0, ours)]
    rest = jnp.concatenate(rest, 1)
    for copy in copies:
        copy.wait()
    total = jnp.dot(left, held[...], preferred_element_type=jnp.float32) + rest
    out[...] = total.astype(out.dtype)


def blend(got, rows_by, swap):
    pairs, rows, _ = got.shape
    count, _, sub, width = rows_by.shape
    scratch = [pltpu.VMEM((pairs * count * sub, width // 2), jnp.bfloat16), pltpu.SemaphoreType.DMA((count, pairs))]
    outs = [jax.ShapeDtypeStruct((rows, width // 2), jnp.bfloat16 if swap else jnp.float32)]
    kernel = functools.partial(blend_kernel, swap)
    return call(kernel, "blend", outs, [VMEM, HBM], [got, rows_by], scratch)[0]


def join_kernel(kept, arrived, blended):
    blended[...] = (kept[...] + arrived[...].astype(jnp.float32)).astype(jnp.bfloat16)


def join(kept, arrived):
    return call(join_kernel, "join", [bfloat(*kept.shape)], [VMEM] * 2, [kept, arrived], places=[LAST])[0]


def shards(tokens, doc_ids, query_one, keyval_one, output_one, query_two, keyval_two, output_two):
    count, ranks = lax.axis_size("inst"), lax.axis_size("tp")
    rows, depth = tokens.shape
    head, piece = query_one.shape[1], keyval_one.shape[1]
    groups = None
    if ranks > GROUP:
        groups = [list(range(low, low + GROUP)) for low in range(0, ranks, GROUP)]

    sent, bound = cut(tokens, output_one, keyval_two.T, count)
    output_all = lax.all_gather(bound, "tp", axis=0)
    mine = exchange(sent, "inst")
    weight = widen(query_one, keyval_one.T)
    own_rows, first = project(mine, weight)
    other_rows, sums = project(other_core(mine), weight, first)
    queries, keyvals_t = finish(exchange(sums, "inst"), norms(tokens), head, piece)
    arrived = slices(output_two, queries, count)
    arrived = [arrived[0]] + [shifted(arrived[d], "inst", d) for d in range(1, count)]
    pieces = aim(arrived, ranks // 2)
    pieces = [pieces[0]] + [shifted(pieces[e], "tp", 2 * e) for e in range(1, ranks // 2)]
    context = first_attend(queries, doc_ids, exchange(keyvals_t, "tp", groups), arrived)
    heads = exchange(context, "tp", core_groups())
    mine, rows_by = keep(exchange(spread(heads), "inst"), output_all, pieces)
    sums = advance(own_rows, other_rows, mine, other_core(mine), output_all, query_two, rows_by)
    rows_by = lax.all_gather(rows_by, "inst", axis=0)

    sent = second_attend(exchange(sums, "inst"), doc_ids, depth, head)
    got = exchange(sent, "tp", core_groups())
    arrived = other_core(blend(got, rows_by, True))
    return join(blend(got, rows_by, False), arrived)


def solution(mesh):
    placed = (
        P("inst", None),
        P(),
        P("inst", "tp"),
        P("inst", "tp"),
        P("tp", "inst"),
        P("inst", "tp"),
        P("inst", "tp"),
        P("tp", "inst"),
    )
    return jax.shard_map(
        shards, mesh=mesh, in_specs=placed, out_specs=P("inst", "tp"), check_vma=False
    )
```

```python
import functools
import math

import jax
import jax.numpy as jnp
from jax import lax
from jax.experimental import pallas as pl
from jax.experimental.pallas import tpu as pltpu
from jax.sharding import PartitionSpec as P

GROUP = 8
EPS = 1e-6
LANES = 128
VMEM = pl.BlockSpec(memory_space=pltpu.VMEM)
HBM = pl.BlockSpec(memory_space=pltpu.MemorySpace.HBM)
LAST = pl.BlockSpec(memory_space=pltpu.VMEM)


def contract(left, right, dims):
    return lax.dot_general(left, right, ((dims[:1], dims[1:]), ((), ())), preferred_element_type=jnp.float32)


def exchange(block, axis, groups=None):
    return lax.all_to_all(block, axis, 0, 0, axis_index_groups=groups)


def other_core(block):
    count = lax.axis_size("tp")
    return lax.ppermute(block, "tp", [(s, s ^ 1) for s in range(count)])


def own_core():
    return lax.rem(lax.axis_index("tp"), 2)


def transposed(block, rows):
    row = lax.broadcasted_iota(jnp.int32, (rows, block.shape[1]), 0)
    column = lax.broadcasted_iota(jnp.int32, (rows, block.shape[1]), 1)
    pick = (row == column).astype(jnp.bfloat16)
    return contract(pick, block, (1, 1)).astype(jnp.bfloat16)


def call(kernel, name, outs, ins, args, scratch=(), places=None):
    places = places or [VMEM] * len(outs)
    held = [value for value, spec in zip([*args, *outs], [*ins, *places]) if spec is VMEM]
    total = sum(math.prod(value.shape) * value.dtype.itemsize for value in held)
    work = sum(math.prod(ref.shape) * ref.dtype.itemsize for ref in scratch if hasattr(ref.dtype, "itemsize"))
    resident = total <= 16 * 2**20
    if resident:
        spaces = [spec.memory_space for spec in ins]
        args = [pltpu.with_memory_space_constraint(value, space) for value, space in zip(args, spaces)]
        outs = [out if spec is LAST else spec.memory_space(out.shape, out.dtype) for out, spec in zip(outs, places)]
        limit = work + 12 * 2**20
    else:
        limit = 56 * 2**20
    return pl.pallas_call(
        kernel,
        out_shape=outs,
        in_specs=ins,
        out_specs=[VMEM if spec is LAST else spec for spec in places],
        scratch_shapes=list(scratch),
        compiler_params=pltpu.CompilerParams(vmem_limit_bytes=limit),
        name=name,
    )(*args)


def bfloat(*shape):
    return jax.ShapeDtypeStruct(shape, jnp.bfloat16)


def shifted(block, axis, distance):
    count = lax.axis_size(axis)
    return lax.ppermute(block, axis, [(s, (s + distance) % count) for s in range(count)])


def core_groups():
    ranks = lax.axis_size("tp")
    return [list(range(core, ranks, 2)) for core in range(2)]


def cut_kernel(tokens, output, keyval, sent, bound, held, sems):
    count, half, width = sent.shape
    head = output.shape[0]
    start = pl.multiple_of(own_core() * half, half)
    copies = [
        pltpu.make_async_copy(output, held.at[pl.ds(0, head), :], sems.at[1, 0]),
        pltpu.make_async_copy(keyval, held.at[pl.ds(head, keyval.shape[0]), :], sems.at[1, 1]),
    ]
    for q in range(count):
        source = tokens.at[pl.ds(start, half), pl.ds(q * width, width)]
        copies.append(pltpu.make_async_copy(source, sent.at[q], sems.at[0, q]))
    for copy in copies:
        copy.start()
    for copy in copies[:2]:
        copy.wait()
    save = pltpu.make_async_copy(held, bound, sems.at[1, 2])
    save.start()
    for copy in copies[2:]:
        copy.wait()
    save.wait()


def cut(tokens, output, keyval, count):
    rows, depth = tokens.shape
    together = (output.shape[0] + keyval.shape[0], output.shape[1])
    outs = [bfloat(count, rows // 2, depth // count), bfloat(*together)]
    scratch = [pltpu.VMEM(together, jnp.bfloat16), pltpu.SemaphoreType.DMA((2, max(3, count)))]
    return call(cut_kernel, "cut", outs, [HBM] * 3, [tokens, output, keyval], scratch, [VMEM, HBM])


def widen_kernel(query, keyval, wide, tall):
    head, piece = query.shape[1], keyval.shape[0]
    wide[:, :head] = query[...]
    tall[:piece, :] = keyval[...]
    tall[piece:, :] = jnp.zeros((LANES - piece, tall.shape[1]), tall.dtype)
    for low in range(0, query.shape[0], LANES):
        block = tall[:, low : low + LANES].astype(jnp.float32)
        wide[low : low + LANES, head:] = jnp.transpose(block).astype(jnp.bfloat16)


def widen(query, keyval):
    depth, head = query.shape
    scratch = [pltpu.VMEM((LANES, depth), jnp.bfloat16)]
    outs = [bfloat(depth, head + LANES)]
    return call(widen_kernel, "widen", outs, [VMEM] * 2, [query, keyval], scratch)[0]


def norm_kernel(tokens, scale, whole, sems):
    pieces = sems.shape[0]
    step = tokens.shape[1] // pieces
    copies = []
    for p in range(pieces):
        columns = pl.ds(p * step, step)
        copies.append(pltpu.make_async_copy(tokens.at[:, columns], whole.at[:, columns], sems.at[p]))
    for copy in copies:
        copy.start()
    total = jnp.zeros((tokens.shape[0], LANES), jnp.float32)
    for p, copy in enumerate(copies):
        copy.wait()
        for low in range(p * step, (p + 1) * step, LANES):
            floats = whole[:, low : low + LANES].astype(jnp.float32)
            total = total + floats * floats
    squares = jnp.sum(total, axis=1, keepdims=True)
    scale[...] = lax.rsqrt(squares / tokens.shape[1] + EPS)


def norms(tokens):
    outs = [jax.ShapeDtypeStruct((tokens.shape[0], 1), jnp.float32)]
    scratch = [pltpu.VMEM(tokens.shape, jnp.bfloat16), pltpu.SemaphoreType.DMA((4,))]
    return call(norm_kernel, "norms", outs, [HBM], [tokens], scratch)[0]


def slice_kernel(shard, queries, *pieces):
    count = len(pieces)
    sub = pieces[0].shape[0]
    for i in range(count):

        @pl.when(lax.axis_index("inst") == i)
        def give():
            for d, piece in enumerate(pieces):
                low = (i + d) % count * sub
                piece[...] = shard[low : low + sub, :]


def slices(shard, queries, count):
    head, width = shard.shape
    return call(slice_kernel, "slices", [bfloat(head // count, width)] * count, [VMEM] * 2, [shard, queries])


def aim_kernel(count, *refs):
    arrived, pieces, held = refs[:count], refs[count:-1], refs[-1]
    for d, block in enumerate(arrived):
        held[lax.rem(lax.axis_index("inst") - d + count, count)] = block[...]
    for e, piece in enumerate(pieces):
        piece[...] = held[lax.rem(lax.axis_index("tp") // 2 + e, len(pieces))]


def aim(arrived, planes):
    shape = arrived[0].shape
    kernel = functools.partial(aim_kernel, len(arrived))
    scratch = [pltpu.VMEM((len(arrived), *shape), jnp.bfloat16)]
    return call(kernel, "aim", [bfloat(*shape)] * planes, [VMEM] * len(arrived), arrived, scratch)


def stack_kernel(*refs):
    for e, piece in enumerate(refs[:-2]):
        refs[-1][e] = piece[...]


def stacked(pieces, block):
    args = [*pieces, block]
    outs = [bfloat(len(pieces), *pieces[0].shape)]
    return call(stack_kernel, "stack", outs, [VMEM] * len(args), args, places=[LAST])[0]


def project_kernel(rows, weight, *refs):
    first, (saved, sums, sem) = refs[:-3], refs[-3:]
    count, half, width = rows.shape
    save = pltpu.make_async_copy(rows, saved, sem)
    save.start()
    hidden = rows[...].reshape(count * half, width)
    total = jnp.dot(hidden, weight[...], preferred_element_type=jnp.float32).astype(jnp.bfloat16)
    core = own_core()
    for q in range(count):
        block = total[q * half : (q + 1) * half]
        if first:
            sums[q, pl.ds(pl.multiple_of(core * half, half), half), :] = first[0][q]
            sums[q, pl.ds(pl.multiple_of((1 - core) * half, half), half), :] = block
        else:
            sums[q] = block
    save.wait()


def project(rows, weight, *first):
    count, half, width = rows.shape
    outs = [bfloat(*rows.shape), bfloat(count, half * (1 + len(first)), weight.shape[1])]
    args = [rows, weight, *first]
    scratch = [pltpu.SemaphoreType.DMA(())]
    return call(project_kernel, "project", outs, [VMEM] * len(args), args, scratch, [HBM, VMEM])


def summed(parts):
    total = parts[0].astype(jnp.float32)
    for part in parts[1:]:
        total = total + part.astype(jnp.float32)
    return total


def finish_kernel(parts, scale, queries, keyvals_t):
    head = queries.shape[1]
    total = summed([parts[q] for q in range(parts.shape[0])]) * scale[...]
    queries[...] = (total[:, :head] * head ** (-0.5)).astype(jnp.bfloat16)
    piece = transposed(total[:, head:].astype(jnp.bfloat16), keyvals_t.shape[1])
    for g in range(keyvals_t.shape[0]):
        keyvals_t[g] = piece


def finish(parts, scale, head, piece):
    rows = parts.shape[1]
    outs = [bfloat(rows, head), bfloat(GROUP, piece, rows)]
    return call(finish_kernel, "finish", outs, [VMEM] * 2, [parts, scale])


def attention(queries, keys_t, values_t, dims, doc_ids, back):
    rows = queries.shape[0]
    at = lax.broadcasted_iota(jnp.int32, (rows, rows), 0)
    key_at = lax.broadcasted_iota(jnp.int32, (rows, rows), 1)
    count = doc_ids.shape[0]
    own = lax.rem(lax.axis_index("inst") - back + count, count)
    docs_row = jnp.broadcast_to(doc_ids[pl.ds(own, 1), :].astype(jnp.float32), (rows, rows))
    docs_column = jnp.sum(jnp.where(at == key_at, docs_row, 0.0), axis=1, keepdims=True)
    allowed = (docs_column == docs_row) & (key_at <= at)
    scores = contract(queries, keys_t, (1, dims[0]))
    scores = jnp.where(allowed, scores, -1e30)
    weights = jnp.exp(scores - jnp.max(scores, axis=1, keepdims=True))
    probabilities = weights / jnp.sum(weights, axis=1, keepdims=True)
    return contract(probabilities.astype(jnp.bfloat16), values_t, (1, dims[1])).astype(jnp.bfloat16)


def first_kernel(queries, doc_ids, pieces, *refs):
    context = refs[-1]
    span = pieces.shape[0] // 2
    keys_t = jnp.concatenate([pieces[g] for g in range(span)], 0)
    values_t = jnp.concatenate([pieces[g] for g in range(span, 2 * span)], 0)
    result = attention(queries[...], keys_t, values_t, (0, 1), doc_ids, 0)
    for z in range(context.shape[0]):
        context[z] = result


def first_attend(queries, doc_ids, pieces, arrived):
    outs = [bfloat(lax.axis_size("tp") // 2, *queries.shape)]
    args = [queries, doc_ids, pieces, *arrived]
    return call(first_kernel, "attend", outs, [VMEM] * len(args), args)[0]


def second_kernel(depth, head, rows, parts, doc_ids, sent):
    wide = 3 * head
    total = summed([parts[q, :rows, :wide] for q in range(parts.shape[0])])
    high = summed([parts[q, rows : rows + 16, :] for q in range(parts.shape[0])])
    across = jnp.broadcast_to(high[0:1] + high[1:2], (rows, parts.shape[2]))
    at = lax.broadcasted_iota(jnp.int32, across.shape, 0)
    lane = lax.broadcasted_iota(jnp.int32, across.shape, 1)
    squares = jnp.sum(jnp.where(at == lane, across, 0.0), axis=1, keepdims=True)
    total = total * lax.rsqrt(squares / depth + EPS)
    queries = (total[:, :head] * head ** (-0.5)).astype(jnp.bfloat16)
    keys = total[:, head : 2 * head].astype(jnp.bfloat16)
    values = total[:, 2 * head :].astype(jnp.bfloat16)
    result = attention(queries, keys, values, (1, 0), doc_ids, 1)
    for z in range(sent.shape[0]):
        sent[z, :, :head] = result
        sent[z, :, head:] = parts[z, :rows, wide:]


def second_attend(parts, doc_ids, depth, head):
    rows = doc_ids.shape[1]
    outs = [bfloat(parts.shape[0], rows, parts.shape[2] - 2 * head)]
    kernel = functools.partial(second_kernel, depth, head, rows)
    return call(kernel, "attend", outs, [VMEM] * 2, [parts, doc_ids])[0]


def spread_kernel(heads, output, sent):
    for q in range(sent.shape[0]):
        sent[q] = heads[...]


def spread(heads, output):
    outs = [bfloat(lax.axis_size("inst"), *heads.shape)]
    return call(spread_kernel, "spread", outs, [VMEM, HBM], [heads, output])[0]


def spans(count):
    return [range(low, min(low + 4, count)) for low in range(0, count, 4)]


def place_contexts(mine, other, left, span):
    _, pairs, rows, head = mine.shape
    core = own_core()
    for source, parity in ((mine, core), (other, 1 - core)):
        for e in range(pairs):
            columns = pl.ds(pl.multiple_of((2 * e + parity) * head, head), head)
            for at, q in enumerate(span):
                left[at * rows : (at + 1) * rows, columns] = source[q, e]


def advance_kernel(step, own_rows, other_rows, mine, other, output, query, rows_by, sums, left, held, tall, hidden, blended, sems):
    count, pairs, rows, head = mine.shape
    width = own_rows.shape[2]
    ranks = 2 * pairs
    core = own_core()
    first = lax.axis_index("tp") // GROUP * GROUP
    copies = []
    for at in range(width // step):
        columns = pl.ds(at * step, step)
        pairs_of = [
            (output.at[:, pl.ds(0, head), columns], held.at[:, :, columns]),
            (own_rows.at[:, :, columns], hidden.at[:, core, :, columns]),
            (other_rows.at[:, :, columns], hidden.at[:, 1 - core, :, columns]),
            (output.at[pl.ds(first, GROUP), pl.ds(head, tall.shape[1]), columns], tall.at[:, :, columns]),
        ]
        copies.append([pltpu.make_async_copy(*pair, sems.at[c, at]) for c, pair in enumerate(pairs_of)])
    for chunk in copies:
        for copy in chunk:
            copy.start()
    for span in spans(count):
        place_contexts(mine, other, left, span)
        low, high = span[0] * rows, (span[-1] + 1) * rows
        queries, keyvals, squares = 0.0, 0.0, jnp.zeros((high - low, LANES), jnp.float32)
        for at, chunk in enumerate(copies):
            if span[0] == 0:
                for copy in chunk:
                    copy.wait()
            columns = pl.ds(at * step, step)
            right = held[:, :, columns].reshape(ranks * head, step)
            attended = jnp.dot(left[: high - low, :], right, preferred_element_type=jnp.float32)
            before = hidden[span[0] : span[-1] + 1, :, :, columns].reshape(high - low, step)
            after_one = (before.astype(jnp.float32) + attended).astype(jnp.bfloat16)
            blended[low:high, columns] = after_one
            queries = queries + jnp.dot(after_one, query[columns, :], preferred_element_type=jnp.float32)
            right = tall[:, :, columns].reshape(GROUP * tall.shape[1], step)
            keyvals = keyvals + contract(after_one, right, (1, 1))
            floats = after_one.astype(jnp.float32)
            for lane in range(0, step, LANES):
                part = floats[:, lane : lane + LANES]
                squares = squares + part * part
        squares = jnp.sum(squares, axis=1, keepdims=True)
        queries, keyvals = queries.astype(jnp.bfloat16), keyvals.astype(jnp.bfloat16)
        for at, q in enumerate(span):
            slot = (q + 1) % count
            block = slice(at * rows, (at + 1) * rows)
            sums[slot, :rows, :head] = queries[block]
            sums[slot, :rows, head : 3 * head] = keyvals[block]
            lanes = sums.shape[2]
            row = lax.broadcasted_iota(jnp.int32, (rows, lanes), 0)
            lane = lax.broadcasted_iota(jnp.int32, (rows, lanes), 1)
            square = jnp.where(row == lane, squares[block], 0.0)
            square = jnp.sum(square, axis=0, keepdims=True)
            high_part = square.astype(jnp.bfloat16).astype(jnp.float32)
            row = lax.broadcasted_iota(jnp.int32, (16, lanes), 0)
            extra = jnp.where(row == 0, high_part, jnp.where(row == 1, square - high_part, 0.0))
            sums[slot, rows:, :] = extra.astype(jnp.bfloat16)
    wide = 3 * head
    slim = (sums.shape[2] - wide) // 2
    for r in range(ranks):

        @pl.when(lax.axis_index("tp") == r)
        def give():
            for b in range(2):
                low = b * (width // 2) + r * slim
                for q in range(count):
                    block = blended[q * rows : (q + 1) * rows, low : low + slim]
                    sums[(q + 1) % count, :rows, wide + b * slim : wide + (b + 1) * slim] = block


def advance(own_rows, other_rows, mine, other, output, query, rows_by):
    count, pairs, rows, head = mine.shape
    width = own_rows.shape[2]
    total = count * rows
    step = min(1024, width)
    ranks, both, _ = output.shape
    scratch = [
        pltpu.VMEM((min(4, count) * rows, ranks * head), jnp.bfloat16),
        pltpu.VMEM((ranks, head, width), jnp.bfloat16),
        pltpu.VMEM((GROUP, both - head, width), jnp.bfloat16),
        pltpu.VMEM((count, 2, rows // 2, width), jnp.bfloat16),
        pltpu.VMEM((total, width), jnp.bfloat16),
        pltpu.SemaphoreType.DMA((4, width // step)),
    ]
    outs = [bfloat(count, rows + 16, 3 * head + width // ranks)]
    ins = [HBM] * 2 + [VMEM] * 2 + [HBM, VMEM, HBM]
    args = [own_rows, other_rows, mine, other, output, query, rows_by]
    return call(functools.partial(advance_kernel, step), "advance", outs, ins, args, scratch)[0]


def blend_kernel(swap, got, rows_by, out, held, sems):
    pairs, rows, _ = got.shape
    count, _, sub, _ = rows_by.shape
    head = count * sub
    plane = lax.axis_index("tp") // 2
    half = out.shape[1]
    slim = half // (2 * pairs)
    core = own_core()
    place = 1 - core if swap else core
    copies = []
    for i in range(count):
        for e in range(pairs):
            source = rows_by.at[i, e, :, pl.ds(pl.multiple_of(place * half, half), half)]
            target = held.at[pl.ds(e * head + i * sub, sub), :]
            copies.append(pltpu.make_async_copy(source, target, sems.at[i, e]))
    for copy in copies:
        copy.start()
    left = jnp.concatenate([got[lax.rem(plane - e + pairs, pairs), :, :head] for e in range(pairs)], 1)
    rest = []
    for a in range(pairs):
        low = got[a, :, head : head + slim]
        high = got[a, :, head + slim : head + 2 * slim]
        ours = jnp.where(place == 0, low, high).astype(jnp.float32)
        rest += [jnp.where(core == 0, ours, 0.0), jnp.where(core == 0, 0.0, ours)]
    rest = jnp.concatenate(rest, 1)
    for copy in copies:
        copy.wait()
    total = jnp.dot(left, held[...], preferred_element_type=jnp.float32) + rest
    out[...] = total.astype(out.dtype)


def blend(got, rows_by, swap):
    pairs, rows, _ = got.shape
    count, _, sub, width = rows_by.shape
    scratch = [pltpu.VMEM((pairs * count * sub, width // 2), jnp.bfloat16), pltpu.SemaphoreType.DMA((count, pairs))]
    outs = [jax.ShapeDtypeStruct((rows, width // 2), jnp.bfloat16 if swap else jnp.float32)]
    kernel = functools.partial(blend_kernel, swap)
    return call(kernel, "blend", outs, [VMEM, HBM], [got, rows_by], scratch)[0]


def join_kernel(kept, arrived, blended):
    blended[...] = (kept[...] + arrived[...].astype(jnp.float32)).astype(jnp.bfloat16)


def join(kept, arrived):
    return call(join_kernel, "join", [bfloat(*kept.shape)], [VMEM] * 2, [kept, arrived], places=[LAST])[0]


def shards(tokens, doc_ids, query_one, keyval_one, output_one, query_two, keyval_two, output_two):
    count, ranks = lax.axis_size("inst"), lax.axis_size("tp")
    rows, depth = tokens.shape
    head, piece = query_one.shape[1], keyval_one.shape[1]
    groups = None
    if ranks > GROUP:
        groups = [list(range(low, low + GROUP)) for low in range(0, ranks, GROUP)]

    sent, bound = cut(tokens, output_one, keyval_two.T, count)
    output_all = lax.all_gather(bound, "tp", axis=0)
    mine = exchange(sent, "inst")
    weight = widen(query_one, keyval_one.T)
    own_rows, first = project(mine, weight)
    other_rows, sums = project(other_core(mine), weight, first)
    queries, keyvals_t = finish(exchange(sums, "inst"), norms(tokens), head, piece)
    arrived = slices(output_two, queries, count)
    arrived = [arrived[0]] + [shifted(arrived[d], "inst", d) for d in range(1, count)]
    pieces = aim(arrived, ranks // 2)
    pieces = [pieces[0]] + [shifted(pieces[e], "tp", 2 * e) for e in range(1, ranks // 2)]
    context = first_attend(queries, doc_ids, exchange(keyvals_t, "tp", groups), arrived)
    heads = exchange(context, "tp", core_groups())
    mine = exchange(spread(heads, output_all), "inst")
    rows_by = stacked(pieces, mine)
    sums = advance(own_rows, other_rows, mine, other_core(mine), output_all, query_two, rows_by)
    rows_by = lax.all_gather(rows_by, "inst", axis=0)

    sent = second_attend(exchange(sums, "inst"), doc_ids, depth, head)
    got = exchange(sent, "tp", core_groups())
    arrived = other_core(blend(got, rows_by, True))
    return join(blend(got, rows_by, False), arrived)


def solution(mesh):
    placed = (
        P("inst", None),
        P(),
        P("inst", "tp"),
        P("inst", "tp"),
        P("tp", "inst"),
        P("inst", "tp"),
        P("inst", "tp"),
        P("tp", "inst"),
    )
    return jax.shard_map(
        shards, mesh=mesh, in_specs=placed, out_specs=P("inst", "tp"), check_vma=False
    )
```

```python
import functools
import math

import jax
import jax.numpy as jnp
from jax import lax
from jax.experimental import pallas as pl
from jax.experimental.pallas import tpu as pltpu
from jax.sharding import PartitionSpec as P

GROUP = 8
EPS = 1e-6
LANES = 128
VMEM = pl.BlockSpec(memory_space=pltpu.VMEM)
HBM = pl.BlockSpec(memory_space=pltpu.MemorySpace.HBM)
LAST = pl.BlockSpec(memory_space=pltpu.VMEM)


def contract(left, right, dims):
    return lax.dot_general(left, right, ((dims[:1], dims[1:]), ((), ())), preferred_element_type=jnp.float32)


def exchange(block, axis, groups=None):
    return lax.all_to_all(block, axis, 0, 0, axis_index_groups=groups)


def other_core(block):
    count = lax.axis_size("tp")
    return lax.ppermute(block, "tp", [(s, s ^ 1) for s in range(count)])


def own_core():
    return lax.rem(lax.axis_index("tp"), 2)


def transposed(block, rows):
    row = lax.broadcasted_iota(jnp.int32, (rows, block.shape[1]), 0)
    column = lax.broadcasted_iota(jnp.int32, (rows, block.shape[1]), 1)
    pick = (row == column).astype(jnp.bfloat16)
    return contract(pick, block, (1, 1)).astype(jnp.bfloat16)


def call(kernel, name, outs, ins, args, scratch=(), places=None):
    places = places or [VMEM] * len(outs)
    held = [value for value, spec in zip([*args, *outs], [*ins, *places]) if spec is VMEM]
    total = sum(math.prod(value.shape) * value.dtype.itemsize for value in held)
    work = sum(math.prod(ref.shape) * ref.dtype.itemsize for ref in scratch if hasattr(ref.dtype, "itemsize"))
    resident = total <= 16 * 2**20
    if resident:
        spaces = [spec.memory_space for spec in ins]
        args = [pltpu.with_memory_space_constraint(value, space) for value, space in zip(args, spaces)]
        outs = [out if spec is LAST else spec.memory_space(out.shape, out.dtype) for out, spec in zip(outs, places)]
        limit = work + 12 * 2**20
    else:
        limit = 56 * 2**20
    return pl.pallas_call(
        kernel,
        out_shape=outs,
        in_specs=ins,
        out_specs=[VMEM if spec is LAST else spec for spec in places],
        scratch_shapes=list(scratch),
        compiler_params=pltpu.CompilerParams(vmem_limit_bytes=limit),
        name=name,
    )(*args)


def bfloat(*shape):
    return jax.ShapeDtypeStruct(shape, jnp.bfloat16)


def shifted(block, axis, distance):
    count = lax.axis_size(axis)
    return lax.ppermute(block, axis, [(s, (s + distance) % count) for s in range(count)])


def core_groups():
    ranks = lax.axis_size("tp")
    return [list(range(core, ranks, 2)) for core in range(2)]


def cut_kernel(tokens, output, keyval, sent, bound, held, sems):
    count, half, width = sent.shape
    head = output.shape[0]
    start = pl.multiple_of(own_core() * half, half)
    copies = [
        pltpu.make_async_copy(output, held.at[pl.ds(0, head), :], sems.at[1, 0]),
        pltpu.make_async_copy(keyval, held.at[pl.ds(head, keyval.shape[0]), :], sems.at[1, 1]),
    ]
    for q in range(count):
        source = tokens.at[pl.ds(start, half), pl.ds(q * width, width)]
        copies.append(pltpu.make_async_copy(source, sent.at[q], sems.at[0, q]))
    for copy in copies:
        copy.start()
    for copy in copies[:2]:
        copy.wait()
    save = pltpu.make_async_copy(held, bound, sems.at[1, 2])
    save.start()
    for copy in copies[2:]:
        copy.wait()
    save.wait()


def cut(tokens, output, keyval, count):
    rows, depth = tokens.shape
    together = (output.shape[0] + keyval.shape[0], output.shape[1])
    outs = [bfloat(count, rows // 2, depth // count), bfloat(*together)]
    scratch = [pltpu.VMEM(together, jnp.bfloat16), pltpu.SemaphoreType.DMA((2, max(3, count)))]
    return call(cut_kernel, "cut", outs, [HBM] * 3, [tokens, output, keyval], scratch, [VMEM, HBM])


def widen_kernel(query, keyval, wide, tall):
    head, piece = query.shape[1], keyval.shape[0]
    wide[:, :head] = query[...]
    tall[:piece, :] = keyval[...]
    tall[piece:, :] = jnp.zeros((LANES - piece, tall.shape[1]), tall.dtype)
    for low in range(0, query.shape[0], LANES):
        block = tall[:, low : low + LANES].astype(jnp.float32)
        wide[low : low + LANES, head:] = jnp.transpose(block).astype(jnp.bfloat16)


def widen(query, keyval):
    depth, head = query.shape
    scratch = [pltpu.VMEM((LANES, depth), jnp.bfloat16)]
    outs = [bfloat(depth, head + LANES)]
    return call(widen_kernel, "widen", outs, [VMEM] * 2, [query, keyval], scratch)[0]


def norm_kernel(tokens, scale, whole, sems):
    pieces = sems.shape[0]
    step = tokens.shape[1] // pieces
    copies = []
    for p in range(pieces):
        columns = pl.ds(p * step, step)
        copies.append(pltpu.make_async_copy(tokens.at[:, columns], whole.at[:, columns], sems.at[p]))
    for copy in copies:
        copy.start()
    total = jnp.zeros((tokens.shape[0], LANES), jnp.float32)
    for p, copy in enumerate(copies):
        copy.wait()
        for low in range(p * step, (p + 1) * step, LANES):
            floats = whole[:, low : low + LANES].astype(jnp.float32)
            total = total + floats * floats
    squares = jnp.sum(total, axis=1, keepdims=True)
    scale[...] = lax.rsqrt(squares / tokens.shape[1] + EPS)


def norms(tokens):
    outs = [jax.ShapeDtypeStruct((tokens.shape[0], 1), jnp.float32)]
    scratch = [pltpu.VMEM(tokens.shape, jnp.bfloat16), pltpu.SemaphoreType.DMA((4,))]
    return call(norm_kernel, "norms", outs, [HBM], [tokens], scratch)[0]


def slice_kernel(shard, queries, *pieces):
    count = len(pieces)
    sub = pieces[0].shape[0]
    for i in range(count):

        @pl.when(lax.axis_index("inst") == i)
        def give():
            for d, piece in enumerate(pieces):
                low = (i + d) % count * sub
                piece[...] = shard[low : low + sub, :]


def slices(shard, queries, count):
    head, width = shard.shape
    return call(slice_kernel, "slices", [bfloat(head // count, width)] * count, [VMEM] * 2, [shard, queries])


def aim_kernel(count, *refs):
    arrived, pieces, held = refs[:count], refs[count:-1], refs[-1]
    for d, block in enumerate(arrived):
        held[lax.rem(lax.axis_index("inst") - d + count, count)] = block[...]
    for e, piece in enumerate(pieces):
        piece[...] = held[lax.rem(lax.axis_index("tp") // 2 + e, len(pieces))]


def aim(arrived, planes):
    shape = arrived[0].shape
    kernel = functools.partial(aim_kernel, len(arrived))
    scratch = [pltpu.VMEM((len(arrived), *shape), jnp.bfloat16)]
    return call(kernel, "aim", [bfloat(*shape)] * planes, [VMEM] * len(arrived), arrived, scratch)


def stack_kernel(*refs):
    for e, piece in enumerate(refs[:-2]):
        refs[-1][e] = piece[...]


def stacked(pieces, block):
    args = [*pieces, block]
    outs = [bfloat(len(pieces), *pieces[0].shape)]
    return call(stack_kernel, "stack", outs, [VMEM] * len(args), args, places=[LAST])[0]


def project_kernel(rows, weight, *refs):
    first, (saved, sums, sem) = refs[:-3], refs[-3:]
    count, half, width = rows.shape
    save = pltpu.make_async_copy(rows, saved, sem)
    save.start()
    hidden = rows[...].reshape(count * half, width)
    total = jnp.dot(hidden, weight[...], preferred_element_type=jnp.float32).astype(jnp.bfloat16)
    core = own_core()
    for q in range(count):
        block = total[q * half : (q + 1) * half]
        if first:
            sums[q, pl.ds(pl.multiple_of(core * half, half), half), :] = first[0][q]
            sums[q, pl.ds(pl.multiple_of((1 - core) * half, half), half), :] = block
        else:
            sums[q] = block
    save.wait()


def project(rows, weight, *first):
    count, half, width = rows.shape
    outs = [bfloat(*rows.shape), bfloat(count, half * (1 + len(first)), weight.shape[1])]
    args = [rows, weight, *first]
    scratch = [pltpu.SemaphoreType.DMA(())]
    return call(project_kernel, "project", outs, [VMEM] * len(args), args, scratch, [HBM, VMEM])


def summed(parts):
    total = parts[0].astype(jnp.float32)
    for part in parts[1:]:
        total = total + part.astype(jnp.float32)
    return total


def finish_kernel(parts, scale, queries, keyvals_t):
    head = queries.shape[1]
    total = summed([parts[q] for q in range(parts.shape[0])]) * scale[...]
    queries[...] = (total[:, :head] * head ** (-0.5)).astype(jnp.bfloat16)
    piece = transposed(total[:, head:].astype(jnp.bfloat16), keyvals_t.shape[1])
    for g in range(keyvals_t.shape[0]):
        keyvals_t[g] = piece


def finish(parts, scale, head, piece):
    rows = parts.shape[1]
    outs = [bfloat(rows, head), bfloat(GROUP, piece, rows)]
    return call(finish_kernel, "finish", outs, [VMEM] * 2, [parts, scale])


def attention(queries, keys_t, values_t, dims, doc_ids, back):
    rows = queries.shape[0]
    at = lax.broadcasted_iota(jnp.int32, (rows, rows), 0)
    key_at = lax.broadcasted_iota(jnp.int32, (rows, rows), 1)
    count = doc_ids.shape[0]
    own = lax.rem(lax.axis_index("inst") - back + count, count)
    docs_row = jnp.broadcast_to(doc_ids[pl.ds(own, 1), :].astype(jnp.float32), (rows, rows))
    docs_column = jnp.sum(jnp.where(at == key_at, docs_row, 0.0), axis=1, keepdims=True)
    allowed = (docs_column == docs_row) & (key_at <= at)
    scores = contract(queries, keys_t, (1, dims[0]))
    scores = jnp.where(allowed, scores, -1e30)
    weights = jnp.exp(scores - jnp.max(scores, axis=1, keepdims=True))
    probabilities = weights / jnp.sum(weights, axis=1, keepdims=True)
    return contract(probabilities.astype(jnp.bfloat16), values_t, (1, dims[1])).astype(jnp.bfloat16)


def first_kernel(queries, doc_ids, pieces, *refs):
    context = refs[-1]
    span = pieces.shape[0] // 2
    keys_t = jnp.concatenate([pieces[g] for g in range(span)], 0)
    values_t = jnp.concatenate([pieces[g] for g in range(span, 2 * span)], 0)
    result = attention(queries[...], keys_t, values_t, (0, 1), doc_ids, 0)
    for z in range(context.shape[0]):
        context[z] = result


def first_attend(queries, doc_ids, pieces, arrived):
    outs = [bfloat(lax.axis_size("tp") // 2, *queries.shape)]
    args = [queries, doc_ids, pieces, *arrived]
    return call(first_kernel, "attend", outs, [VMEM] * len(args), args)[0]


def second_kernel(depth, head, rows, parts, doc_ids, sent):
    wide = 3 * head
    total = summed([parts[q, :rows, :wide] for q in range(parts.shape[0])])
    high = summed([parts[q, rows : rows + 16, :] for q in range(parts.shape[0])])
    across = jnp.broadcast_to(high[0:1] + high[1:2], (rows, parts.shape[2]))
    at = lax.broadcasted_iota(jnp.int32, across.shape, 0)
    lane = lax.broadcasted_iota(jnp.int32, across.shape, 1)
    squares = jnp.sum(jnp.where(at == lane, across, 0.0), axis=1, keepdims=True)
    total = total * lax.rsqrt(squares / depth + EPS)
    queries = (total[:, :head] * head ** (-0.5)).astype(jnp.bfloat16)
    keys = total[:, head : 2 * head].astype(jnp.bfloat16)
    values = total[:, 2 * head :].astype(jnp.bfloat16)
    result = attention(queries, keys, values, (1, 0), doc_ids, 1)
    for z in range(sent.shape[0]):
        sent[z, :, :head] = result
        sent[z, :, head:] = parts[z, :rows, wide:]


def second_attend(parts, doc_ids, depth, head):
    rows = doc_ids.shape[1]
    outs = [bfloat(parts.shape[0], rows, parts.shape[2] - 2 * head)]
    kernel = functools.partial(second_kernel, depth, head, rows)
    return call(kernel, "attend", outs, [VMEM] * 2, [parts, doc_ids])[0]


def spread_kernel(heads, output, sent):
    for q in range(sent.shape[0]):
        sent[q] = heads[...]


def spread(heads, output):
    outs = [bfloat(lax.axis_size("inst"), *heads.shape)]
    return call(spread_kernel, "spread", outs, [VMEM, HBM], [heads, output])[0]


def spans(count):
    return [range(low, min(low + 4, count)) for low in range(0, count, 4)]


def place_contexts(mine, other, left, span):
    _, pairs, rows, head = mine.shape
    core = own_core()
    for source, parity in ((mine, core), (other, 1 - core)):
        for e in range(pairs):
            columns = pl.ds(pl.multiple_of((2 * e + parity) * head, head), head)
            for at, q in enumerate(span):
                left[at * rows : (at + 1) * rows, columns] = source[q, e]


def advance_kernel(step, own_rows, other_rows, mine, other, output, query, rows_by, sums, left, held, tall, hidden, blended, sems):
    count, pairs, rows, head = mine.shape
    width = own_rows.shape[2]
    ranks = 2 * pairs
    core = own_core()
    first = lax.axis_index("tp") // GROUP * GROUP
    copies = []
    for at in range(width // step):
        columns = pl.ds(at * step, step)
        pairs_of = [
            (output.at[:, pl.ds(0, head), columns], held.at[:, :, columns]),
            (own_rows.at[:, :, columns], hidden.at[:, core, :, columns]),
            (other_rows.at[:, :, columns], hidden.at[:, 1 - core, :, columns]),
            (output.at[pl.ds(first, GROUP), pl.ds(head, tall.shape[1]), columns], tall.at[:, :, columns]),
        ]
        copies.append([pltpu.make_async_copy(*pair, sems.at[c, at]) for c, pair in enumerate(pairs_of)])
    for chunk in copies:
        for copy in chunk:
            copy.start()
    for span in spans(count):
        place_contexts(mine, other, left, span)
        low, high = span[0] * rows, (span[-1] + 1) * rows
        queries, keyvals, squares = 0.0, 0.0, jnp.zeros((high - low, LANES), jnp.float32)
        for at, chunk in enumerate(copies):
            if span[0] == 0:
                for copy in chunk:
                    copy.wait()
            columns = pl.ds(at * step, step)
            right = held[:, :, columns].reshape(ranks * head, step)
            attended = jnp.dot(left[: high - low, :], right, preferred_element_type=jnp.float32)
            before = hidden[span[0] : span[-1] + 1, :, :, columns].reshape(high - low, step)
            after_one = (before.astype(jnp.float32) + attended).astype(jnp.bfloat16)
            blended[low:high, columns] = after_one
            queries = queries + jnp.dot(after_one, query[columns, :], preferred_element_type=jnp.float32)
            right = tall[:, :, columns].reshape(GROUP * tall.shape[1], step)
            keyvals = keyvals + contract(after_one, right, (1, 1))
            floats = after_one.astype(jnp.float32)
            for lane in range(0, step, LANES):
                part = floats[:, lane : lane + LANES]
                squares = squares + part * part
        squares = jnp.sum(squares, axis=1, keepdims=True)
        queries, keyvals = queries.astype(jnp.bfloat16), keyvals.astype(jnp.bfloat16)
        for at, q in enumerate(span):
            slot = (q + 1) % count
            block = slice(at * rows, (at + 1) * rows)
            sums[slot, :rows, :head] = queries[block]
            sums[slot, :rows, head : 3 * head] = keyvals[block]
            lanes = sums.shape[2]
            row = lax.broadcasted_iota(jnp.int32, (rows, lanes), 0)
            lane = lax.broadcasted_iota(jnp.int32, (rows, lanes), 1)
            square = jnp.where(row == lane, squares[block], 0.0)
            square = jnp.sum(square, axis=0, keepdims=True)
            high_part = square.astype(jnp.bfloat16).astype(jnp.float32)
            row = lax.broadcasted_iota(jnp.int32, (16, lanes), 0)
            extra = jnp.where(row == 0, high_part, jnp.where(row == 1, square - high_part, 0.0))
            sums[slot, rows:, :] = extra.astype(jnp.bfloat16)
    wide = 3 * head
    slim = (sums.shape[2] - wide) // 2
    for r in range(ranks):

        @pl.when(lax.axis_index("tp") == r)
        def give():
            for b in range(2):
                low = b * (width // 2) + r * slim
                for q in range(count):
                    block = blended[q * rows : (q + 1) * rows, low : low + slim]
                    sums[(q + 1) % count, :rows, wide + b * slim : wide + (b + 1) * slim] = block


def advance(own_rows, other_rows, mine, other, output, query, rows_by):
    count, pairs, rows, head = mine.shape
    width = own_rows.shape[2]
    total = count * rows
    step = min(1024, width)
    ranks, both, _ = output.shape
    scratch = [
        pltpu.VMEM((min(4, count) * rows, ranks * head), jnp.bfloat16),
        pltpu.VMEM((ranks, head, width), jnp.bfloat16),
        pltpu.VMEM((GROUP, both - head, width), jnp.bfloat16),
        pltpu.VMEM((count, 2, rows // 2, width), jnp.bfloat16),
        pltpu.VMEM((total, width), jnp.bfloat16),
        pltpu.SemaphoreType.DMA((4, width // step)),
    ]
    outs = [bfloat(count, rows + 16, 3 * head + width // ranks)]
    ins = [HBM] * 2 + [VMEM] * 2 + [HBM, VMEM, HBM]
    args = [own_rows, other_rows, mine, other, output, query, rows_by]
    return call(functools.partial(advance_kernel, step), "advance", outs, ins, args, scratch)[0]


def blend_kernel(swap, got, rows_by, out, held, sems):
    pairs, rows, _ = got.shape
    count, _, sub, _ = rows_by.shape
    head = count * sub
    plane = lax.axis_index("tp") // 2
    half = out.shape[1]
    slim = half // (2 * pairs)
    core = own_core()
    place = 1 - core if swap else core
    copies = []
    for i in range(count):
        for e in range(pairs):
            source = rows_by.at[i, e, :, pl.ds(pl.multiple_of(place * half, half), half)]
            target = held.at[pl.ds(e * head + i * sub, sub), :]
            copies.append(pltpu.make_async_copy(source, target, sems.at[i, e]))
    for copy in copies:
        copy.start()
    left = jnp.concatenate([got[lax.rem(plane - e + pairs, pairs), :, :head] for e in range(pairs)], 1)
    rest = []
    for a in range(pairs):
        low = got[a, :, head : head + slim]
        high = got[a, :, head + slim : head + 2 * slim]
        ours = jnp.where(place == 0, low, high).astype(jnp.float32)
        rest += [jnp.where(core == 0, ours, 0.0), jnp.where(core == 0, 0.0, ours)]
    rest = jnp.concatenate(rest, 1)
    for copy in copies:
        copy.wait()
    total = jnp.dot(left, held[...], preferred_element_type=jnp.float32) + rest
    out[...] = total.astype(out.dtype)


def blend(got, rows_by, swap):
    pairs, rows, _ = got.shape
    count, _, sub, width = rows_by.shape
    scratch = [pltpu.VMEM((pairs * count * sub, width // 2), jnp.bfloat16), pltpu.SemaphoreType.DMA((count, pairs))]
    outs = [jax.ShapeDtypeStruct((rows, width // 2), jnp.bfloat16 if swap else jnp.float32)]
    kernel = functools.partial(blend_kernel, swap)
    return call(kernel, "blend", outs, [VMEM, HBM], [got, rows_by], scratch)[0]


def join_kernel(kept, arrived, blended):
    blended[...] = (kept[...] + arrived[...].astype(jnp.float32)).astype(jnp.bfloat16)


def join(kept, arrived):
    return call(join_kernel, "join", [bfloat(*kept.shape)], [VMEM] * 2, [kept, arrived], places=[LAST])[0]


def shards(tokens, doc_ids, query_one, keyval_one, output_one, query_two, keyval_two, output_two):
    count, ranks = lax.axis_size("inst"), lax.axis_size("tp")
    rows, depth = tokens.shape
    head, piece = query_one.shape[1], keyval_one.shape[1]
    groups = None
    if ranks > GROUP:
        groups = [list(range(low, low + GROUP)) for low in range(0, ranks, GROUP)]

    sent, bound = cut(tokens, output_one, keyval_two.T, count)
    output_all = lax.all_gather(bound, "tp", axis=0)
    mine = exchange(sent, "inst")
    weight = widen(query_one, keyval_one.T)
    own_rows, first = project(mine, weight)
    other_rows, sums = project(other_core(mine), weight, first)
    queries, keyvals_t = finish(exchange(sums, "inst"), norms(tokens), head, piece)
    arrived = slices(output_two, queries, count)
    arrived = [arrived[0]] + [shifted(arrived[d], "inst", d) for d in range(1, count)]
    pieces = aim(arrived, ranks // 2)
    pieces = [pieces[0]] + [shifted(pieces[e], "tp", 2 * e) for e in range(1, ranks // 2)]
    context = first_attend(queries, doc_ids, exchange(keyvals_t, "tp", groups), arrived)
    heads = exchange(context, "tp", core_groups())
    mine = exchange(spread(heads, output_all), "inst")
    other = other_core(mine)
    rows_by = stacked(pieces, other)
    sums = advance(own_rows, other_rows, mine, other, output_all, query_two, rows_by)
    rows_by = lax.all_gather(rows_by, "inst", axis=0)

    sent = second_attend(exchange(sums, "inst"), doc_ids, depth, head)
    got = exchange(sent, "tp", core_groups())
    arrived = other_core(blend(got, rows_by, True))
    return join(blend(got, rows_by, False), arrived)


def solution(mesh):
    placed = (
        P("inst", None),
        P(),
        P("inst", "tp"),
        P("inst", "tp"),
        P("tp", "inst"),
        P("inst", "tp"),
        P("inst", "tp"),
        P("tp", "inst"),
    )
    return jax.shard_map(
        shards, mesh=mesh, in_specs=placed, out_specs=P("inst", "tp"), check_vma=False
    )
```
